512 devices in a mesh: leaf: 16 (over z), row: 8 (over x, core), col: 4 (over y).
Axes of the slice: x: 4, y: 4, z: 16, core: 2. Of those that a mesh axis runs over, the one named last changes fastest.
Arguments:
- pivot: float32 [16, 1024, 1024], P('leaf', 'row', 'col'), as said below
- border: float32 [16, 3072, 1024], P('leaf', 'row', 'col'), may hold values from -0.065625 to 0.065625
- update: float32 [16, 3072, 3072], P('leaf', 'row', 'col'), as said below
- child_map: int32 [16, 3072], replicated, may hold values from 0 to 4607, as said below
- parent_diag: float32 [16, 2304], P('leaf', 'row'), may hold values from 0.5 to 4
Outputs:
- factor_pivot: float32 [16, 1024, 1024], P('leaf', 'row', 'col')
- factor_border: float32 [16, 3072, 1024], P('leaf', 'row', 'col')
- parent_front: float32 [16, 2304, 4608], P('leaf', 'row', 'col')
The draws below stay inside these ranges and needn't reach their ends.
Inputs may be any that keep to these rules, and one draw needn't show every extreme that they name: Each row child_map[l] is increasing with distinct entries, and its i-th block of 384 entries lies among parent rows i * 576 to (i+1) * 576 - 1. Each pivot[l] is symmetric positive definite. Each update[l] is symmetric.
All inputs are finite; a program needn't handle non-finite values.
Results may differ from the reference program's by a relative error of at most 0.00007.
Values sent between devices are 32-bit elements; how exact they have to be, the bound alone decides.
No kernel may reach another device: no remote copies, remote signals or barrier semaphores. Data moves between devices by JAX's collectives and lax.ppermute only.
A program may use at most 128 MiB of HBM per device.

```python
import math
import jax
import jax.numpy as jnp
from jax import lax

PANEL = 1024
UPD = 3072
PARENT = 4608
CHILD = 4096
LEAVES = 16
NB = 8
RB = 288
N_ROW = 8


def symmetric_part(key, count, order):
    noise = jax.random.normal(key, (count, order, order), jnp.float32)
    return (noise + jnp.swapaxes(noise, 1, 2)) * (0.7 / math.sqrt(2.0 * CHILD))


def dominant(key, order):
    first, second = jax.random.split(key)
    diagonal = jax.random.uniform(second, (LEAVES, order), jnp.float32, 2.0, 4.0)
    return symmetric_part(first, LEAVES, order) + diagonal[:, :, None] * jnp.eye(order, dtype=jnp.float32)[None]


def coupling(key, order):
    places = jnp.arange(order, dtype=jnp.float32)
    distance = jnp.abs(places[:, None] - places[None, :])
    kernel = (3.0 + 6.0 * jnp.exp(-distance * (4.0 / order))) / order
    strength = jax.random.uniform(key, (LEAVES,), jnp.float32, 0.8, 1.6)
    return strength[:, None, None] * kernel[None]


def draw_pivot(key, part):
    base = dominant(jax.random.fold_in(key, 11), PANEL)
    return base + coupling(jax.random.fold_in(key, 19), PANEL)


def draw_update(key, part):
    return dominant(jax.random.fold_in(key, 13), UPD)


def draw_child_map(key, part):
    keys = jax.random.split(jax.random.fold_in(key, 17), LEAVES * NB)

    def choose(single):
        return jnp.sort(jax.random.permutation(single, PARENT // NB)[:UPD // NB])
    picked = jax.vmap(choose)(keys).reshape(LEAVES, NB, UPD // NB)
    offsets = (jnp.arange(NB, dtype=jnp.int32) * (PARENT // NB))[None, :, None]
    return (picked.astype(jnp.int32) + offsets).reshape(LEAVES, UPD).astype(jnp.int32)


def block_scale(key, extent, cuts, least, largest):
    gain = 1.0
    for dim, blocks in cuts:
        heights = jax.random.uniform(jax.random.fold_in(jax.random.fold_in(key, 6), dim), (blocks,), jnp.float32, least / len(cuts), largest / len(cuts))
        gain = gain * jnp.repeat(jnp.exp(heights), extent[dim] // blocks).reshape((-1,) + (1,) * (len(extent) - 1 - dim))
    return gain


def bell_draw(key, shape, spread, bound, cuts=(), held_as=jnp.bfloat16):
    array = jax.random.normal(key, shape, jnp.float32) * spread
    if len(cuts) > 0:
        array = block_scale(key, shape, cuts, -0.22, 0.18) * array
    return jnp.clip(array, min=-bound, max=bound).astype(held_as)


def setup_inputs(seed: int = 0) -> dict:
    splits = jax.random.split(jax.random.key(seed), 6)
    return {
        "pivot": draw_pivot(jax.random.fold_in(splits[5], 71), 0),
        "border": bell_draw(splits[1], (LEAVES, UPD, PANEL), (0.7 / (CHILD ** 0.5)), 0.065625, ((0, 16), (1, 8), (2, 4)), jnp.float32),
        "update": draw_update(jax.random.fold_in(splits[5], 71), 0),
        "child_map": draw_child_map(jax.random.fold_in(splits[5], 71), 0),
        "parent_diag": jnp.clip(jnp.exp(math.log(4.0) - 2.0794415 * jax.random.uniform(splits[4], (LEAVES, PARENT // 2), jnp.float32) ** block_scale(splits[4], (LEAVES, PARENT // 2), ((0, 16), (1, 8)), -0.2, 0.2)), 0.5, 4.0),
    }


def eliminate(blocks):
    piv, bord, upd = blocks
    lower = jnp.linalg.cholesky(piv)
    below = lax.linalg.triangular_solve(lower, bord, left_side=False, lower=True, transpose_a=True)
    schur = upd - jnp.dot(below.astype(jnp.float32), below.T.astype(jnp.float32), precision=lax.Precision.HIGHEST, preferred_element_type=jnp.float32)
    return (lower, below, schur)

def reference(pivot, border, update, child_map, parent_diag):
    lowers, belows, schurs = lax.map(eliminate, (pivot, border, update))
    fronts = []
    for pair in range(LEAVES // 2):
        front = jnp.zeros((PARENT, PARENT), jnp.float32)
        for side in range(2):
            index = child_map[2 * pair + side]
            front = front.at[index[:, None], index[None, :]].add(schurs[2 * pair + side])
        diag_rows = parent_diag[2 * pair:2 * pair + 2].reshape(2, N_ROW, RB).transpose(1, 0, 2).reshape(PARENT)
        front = front + jnp.diag(diag_rows)
        fronts.append(front.reshape(N_ROW, 2, RB, PARENT).transpose(1, 0, 2, 3).reshape(2, PARENT // 2, PARENT))
    return (lowers, belows, jnp.concatenate(fronts, axis=0))
```

```python
import jax
import jax.numpy as jnp
from jax import lax
from jax.experimental import pallas as pl
from jax.experimental.pallas import tpu as pltpu
from jax.sharding import PartitionSpec as P

HI = lax.Precision.HIGHEST
F32 = jnp.float32
BF16 = jnp.bfloat16
B = 128
SB = 32
H = 64
PAYLOAD = 160
VMEM = pl.BlockSpec(memory_space=pltpu.VMEM)
SMEM = pl.BlockSpec(memory_space=pltpu.SMEM)


def dot_tn(a, b, precision=HI):
    return lax.dot_general(a, b, (((0,), (0,)), ((), ())), precision=precision, preferred_element_type=F32)


def dot_nn(a, b, precision=HI):
    return lax.dot_general(a, b, (((1,), (0,)), ((), ())), precision=precision, preferred_element_type=F32)


def dot_nt(a, b, precision=HI):
    return lax.dot_general(a, b, (((1,), (1,)), ((), ())), precision=precision, preferred_element_type=F32)


def params(flops):
    return dict(
        compiler_params=pltpu.CompilerParams(vmem_limit_bytes=48 * 2**20),
        cost_estimate=pl.CostEstimate(flops=flops, bytes_accessed=2**23, transcendentals=0),
    )


def pack_kernel(idx_ref, p_ref, o_ref):
    row, col = idx_ref[0], idx_ref[1]
    copies = o_ref.shape[0]

    def put(lo, value):
        for q in range(copies):
            o_ref[q, lo : lo + value.shape[0], 0 : value.shape[1]] = value

    for half in range(2):
        block = p_ref[:, half * B : half * B + B]
        other = 2 * col + half

        @pl.when(row <= other)
        def _():
            put(half * H, block[0:H, :])

        @pl.when(row > other)
        def _():
            put(half * H, block[:, H:B].T)

        @pl.when(row == other)
        def _():
            corner = block[H:B, H:B]
            put(2 * H, jnp.concatenate([corner[0:32], corner[32:64]], axis=1))


def unpack(src, parity, u_ref, nrow, ncol):
    for x in range(nrow // 2):
        i = 2 * x + parity
        for y in range(ncol):
            c = x * ncol + y
            for half in range(2):
                o = 2 * y + half
                piece = src[c, half * H : half * H + H, :]
                if i <= o:
                    u_ref[i * B : i * B + H, o * B : o * B + B] = piece
                else:
                    u_ref[o * B + H : o * B + B, i * B : i * B + B] = piece
                if i == o:
                    corner = src[c, 2 * H : 2 * H + 32, :]
                    low = jnp.concatenate([corner[:, 0:H], corner[:, H:B]], axis=0)
                    u_ref[i * B + H : i * B + B, i * B : i * B + B] = jnp.concatenate(
                        [piece[:, H:B].T, low], axis=1
                    )


def spread_row(value, r):
    return jnp.broadcast_to(value[r : r + 1, :], (8, B))


def chain(s_ref, s):
    nb, r0 = SB // 8, s * SB
    rowid = lax.broadcasted_iota(jnp.int32, (8, B), 0)
    blk = [s_ref[r0 + 8 * b : r0 + 8 * b + 8, 0:B] for b in range(nb)]
    c = [
        [
            jnp.broadcast_to(blk[b][:, r0 + i : r0 + i + 1], (8, B)) if b >= i // 8 else None
            for b in range(nb)
        ]
        for i in range(SB)
    ]
    x = [[s_ref[r0 + 8 * b : r0 + 8 * b + 8, B * h : B * h + B] for h in range(2)] for b in range(nb)]
    pivots = [None] * nb
    for j in range(SB):
        bj, rj = j // 8, j % 8
        p = spread_row(c[j][bj], rj)
        inv = 1.0 / p
        pivots[bj] = p if pivots[bj] is None else jnp.where(rowid == rj, p, pivots[bj])
        for i in range(j + 1, SB):
            m = spread_row(c[j][i // 8], i % 8) * inv
            for b in range(i // 8, nb):
                c[i][b] = c[i][b] - c[j][b] * m
        for h in range(2):
            xr = spread_row(x[bj][h], rj) * inv
            for b in range(bj, nb):
                cm = c[j][b] if b > bj else jnp.where(rowid > rj, c[j][b], 0.0)
                x[b][h] = x[b][h] - cm * xr
    out = []
    for b in range(nb):
        q = lax.rsqrt(pivots[b])
        out.append(jnp.concatenate([x[b][0] * q, x[b][1] * q], axis=1))
    return jnp.concatenate(out, axis=0)


def factor_block(s_ref):
    for s in range(B // SB):
        p = chain(s_ref, s)
        s_ref[SB * s : SB * s + SB, :] = p
        lo = SB * (s + 1)
        if lo < B:
            s_ref[lo:, :] = s_ref[lo:, :] - dot_tn(p[:, lo:B], p)


def chol_kernel(idx_ref, mine_ref, other_ref, u_ref, w_ref, l_ref, s_ref):
    row, col, core = idx_ref[0], idx_ref[1], idx_ref[2]
    n = u_ref.shape[0]
    nblk = n // B
    ncol = n // l_ref.shape[1]

    for parity in range(2):

        @pl.when(core == parity)
        def _():
            unpack(mine_ref, parity, u_ref, nblk, ncol)
            unpack(other_ref, 1 - parity, u_ref, nblk, ncol)

    ri = lax.broadcasted_iota(jnp.int32, (B, B), 0)
    ci = lax.broadcasted_iota(jnp.int32, (B, B), 1)
    eye = (ri == ci).astype(F32)

    def body(k, _):
        r0 = pl.multiple_of(k * B, B)
        s_ref[:, 0:B] = u_ref[pl.ds(r0, B), pl.ds(r0, B)]
        s_ref[:, B : 2 * B] = eye
        factor_block(s_ref)
        w = s_ref[:, B : 2 * B]
        for kk in range(nblk):

            @pl.when(k == kk)
            def _():
                lo = (kk + 1) * B
                u_ref[kk * B : lo, kk * B : lo] = jnp.where(ri <= ci, s_ref[:, 0:B], 0.0)
                pair = kk // 2
                if kk % 2 == 0:
                    w_ref[pair, 0:B, 0:B] = w
                    w_ref[pair, 0:B, B : 2 * B] = jnp.zeros((B, B), F32)
                else:
                    w_ref[pair, B : 2 * B, B : 2 * B] = w
                    cross = dot_tn(u_ref[(kk - 1) * B : kk * B, kk * B : lo], w_ref[pair, 0:B, 0:B])
                    w_ref[pair, B : 2 * B, 0:B] = -dot_nn(w, cross)
                if lo < n:
                    panel = dot_nn(w, u_ref[kk * B : lo, lo:])
                    u_ref[kk * B : lo, lo:] = panel
                    t = lo
                    while t < n:
                        m = min(256, n - t)
                        u_ref[t : t + m, t:] = u_ref[t : t + m, t:] - dot_tn(
                            panel[:, t - lo : t - lo + m], panel[:, t - lo :]
                        )
                        t += m

        return 0

    lax.fori_loop(0, nblk, body, 0)
    rows, cols = l_ref.shape
    part = u_ref[pl.ds(pl.multiple_of(col * cols, B), cols), pl.ds(pl.multiple_of(row * rows, B), rows)].T
    rl = lax.broadcasted_iota(jnp.int32, (rows, cols), 0) + row * rows
    cl = lax.broadcasted_iota(jnp.int32, (rows, cols), 1) + col * cols
    l_ref[...] = jnp.where(rl >= cl, part, 0.0)


def split3(value):
    first = value.astype(BF16)
    rest = value - first.astype(F32)
    second = rest.astype(BF16)
    third = (rest - second.astype(F32)).astype(BF16)
    return first, second, third


def pick_rows(onehot, value):
    return sum(dot_nn(onehot, part, None) for part in reversed(split3(value)))


def pick_cols(value, onehot):
    return sum(dot_nt(part, onehot, None) for part in reversed(split3(value)))


def solve_kernel(idx_ref, own_ref, mine_ref, other_ref, u_ref, w_ref, upd_ref, map_ref, fb_ref, keep_ref, send_ref, x_ref):
    row, col, core, side = idx_ref[0], idx_ref[1], idx_ref[2], idx_ref[3]
    ncol, rows, width = own_ref.shape
    n = ncol * width
    for y in range(ncol):
        x_ref[0:rows, y * width : (y + 1) * width] = own_ref[y]
        x_ref[pl.ds((1 + core) * rows, rows), y * width : (y + 1) * width] = mine_ref[y]
        x_ref[pl.ds((2 - core) * rows, rows), y * width : (y + 1) * width] = other_ref[y]
    for k in range(ncol):
        lo, hi = k * width, (k + 1) * width
        f = dot_nt(x_ref[:, lo:hi], w_ref[k])
        x_ref[:, lo:hi] = f
        if hi < n:
            x_ref[:, hi:] = x_ref[:, hi:] - dot_nn(f, u_ref[lo:hi, hi:])
    fb_ref[...] = x_ref[0:rows, pl.ds(pl.multiple_of(col * width, B), width)]
    schur = upd_ref[...] - dot_nt(x_ref[0:rows, :], x_ref[rows:, :])
    half = keep_ref.shape[0]
    place = lax.broadcasted_iota(jnp.int32, (half, rows), 0) + row * 2 * half
    for ref, which in ((send_ref, 1 - side), (keep_ref, side)):
        onehot = (place + which * half == map_ref[...]).astype(F32).astype(BF16)
        ref[...] = pick_rows(onehot, schur)


def widen(value, map_ref, first, base):
    blocks, rows = map_ref.shape
    width = value.shape[1] // blocks
    total = first.shape[1]
    step = total // blocks
    for b in range(blocks):
        lo = b * step // B * B
        hi = -((-(b + 1) * step) // B) * B
        place = lax.broadcasted_iota(jnp.int32, (hi - lo, width), 0) + (lo + base)
        onehot = (place == map_ref[b : b + 1, :]).astype(F32).astype(BF16)
        first[:, lo:hi] = first[:, lo:hi] + pick_cols(value[:, b * width : (b + 1) * width], onehot)


def own_kernel(idx_ref, keep_ref, map_ref, diag_ref, o_ref):
    row, col, side = idx_ref[0], idx_ref[1], idx_ref[3]
    half, total = o_ref.shape
    rid = lax.broadcasted_iota(jnp.int32, (half, total), 0) + (row * 2 + side) * half
    cid = lax.broadcasted_iota(jnp.int32, (half, total), 1) + col * total
    o_ref[...] = jnp.where(rid == cid, diag_ref[...], 0.0)
    widen(keep_ref[...], map_ref, o_ref, col * total)


def add_kernel(idx_ref, got_ref, map_ref, base_ref, o_ref):
    o_ref[...] = base_ref[...]
    widen(got_ref[...], map_ref, o_ref, idx_ref[1] * o_ref.shape[1])


def on_device(pivot, border, update, child_map, parent_diag):
    nrow, ncol = lax.axis_size("row"), lax.axis_size("col")
    row, col, leaf = lax.axis_index("row"), lax.axis_index("col"), lax.axis_index("leaf")
    nx = nrow // 2
    core, side = row % 2, leaf % 2
    idx = jnp.stack([row, col, core, side]).astype(jnp.int32)
    piece_rows, piece_cols = pivot.shape[1:]
    n = piece_rows * nrow
    rows, width = border.shape[1:]
    half = parent_diag.shape[1]
    total = 2 * half * nrow // ncol
    upd_cols = update.shape[2]

    chips = nx * ncol
    packed = pl.pallas_call(
        pack_kernel,
        out_shape=jax.ShapeDtypeStruct((chips, PAYLOAD, B), F32),
        in_specs=[SMEM, VMEM],
        out_specs=VMEM,
        **params(10**6),
    )(idx, pivot[0])
    groups = [[(2 * x + c) * ncol + y for x in range(nx) for y in range(ncol)] for c in range(2)]
    mine = lax.all_to_all(packed, ("row", "col"), 0, 0, axis_index_groups=groups, tiled=True)
    swap = [(r, r ^ 1) for r in range(nrow)]
    other = lax.ppermute(mine, "row", swap)

    own_rows = lax.all_gather(border[0], "col", axis=0)
    turn = [((2 * x + c) * ncol + y, (2 * y + c) * ncol + x) for x in range(nx) for c in range(2) for y in range(ncol)]
    turned = lax.ppermute(border[0], ("row", "col"), turn)
    same = [[2 * x + c for x in range(nx)] for c in range(2)]
    col_rows = lax.all_gather(turned, "row", axis=0, axis_index_groups=same)

    upper, inverse, pivot_out = pl.pallas_call(
        chol_kernel,
        out_shape=(
            jax.ShapeDtypeStruct((n, n), F32),
            jax.ShapeDtypeStruct((n // (2 * B), 2 * B, 2 * B), F32),
            jax.ShapeDtypeStruct((piece_rows, piece_cols), F32),
        ),
        in_specs=[SMEM, VMEM, VMEM],
        out_specs=(VMEM, VMEM, VMEM),
        scratch_shapes=[pltpu.VMEM((B, 2 * B), F32)],
        **params(4 * 10**10),
    )(idx, mine, other)
    other_rows = lax.ppermute(col_rows, "row", swap)

    maps = lax.dynamic_slice(child_map, (leaf, row * rows), (1, rows))
    border_out, keep, send = pl.pallas_call(
        solve_kernel,
        out_shape=(
            jax.ShapeDtypeStruct((rows, width), F32),
            jax.ShapeDtypeStruct((half, upd_cols), F32),
            jax.ShapeDtypeStruct((half, upd_cols), F32),
        ),
        in_specs=[SMEM] + [VMEM] * 7,
        out_specs=(VMEM, VMEM, VMEM),
        scratch_shapes=[pltpu.VMEM((3 * rows, n), F32)],
        **params(10**10),
    )(idx, own_rows, col_rows, other_rows, upper, inverse, update[0], maps)

    got = lax.ppermute(send, "leaf", [(s, s ^ 1) for s in range(lax.axis_size("leaf"))])
    blocks = upd_cols // rows

    def col_maps(which):
        return lax.dynamic_slice(child_map, (which, col * upd_cols), (1, upd_cols)).reshape(blocks, rows)

    base = pl.pallas_call(
        own_kernel,
        out_shape=jax.ShapeDtypeStruct((half, total), F32),
        in_specs=[SMEM] + [VMEM] * 3,
        out_specs=VMEM,
        **params(2 * 10**9),
    )(idx, keep, col_maps(leaf), parent_diag.reshape(half, 1))
    parent_out = pl.pallas_call(
        add_kernel,
        out_shape=jax.ShapeDtypeStruct((half, total), F32),
        in_specs=[SMEM] + [VMEM] * 3,
        out_specs=VMEM,
        **params(2 * 10**9),
    )(idx, got, col_maps(leaf ^ 1), base)
    return pivot_out[None], border_out[None], parent_out[None]


def solution(mesh):
    placed = (
        P("leaf", "row", "col"),
        P("leaf", "row", "col"),
        P("leaf", "row", "col"),
        P(),
        P("leaf", "row"),
    )
    return jax.shard_map(
        on_device,
        mesh=mesh,
        in_specs=placed,
        out_specs=(P("leaf", "row", "col"), P("leaf", "row", "col"), P("leaf", "row", "col")),
        check_vma=False,
    )
```

```python
import jax
import jax.numpy as jnp
from jax import lax
from jax.experimental import pallas as pl
from jax.experimental.pallas import tpu as pltpu
from jax.sharding import PartitionSpec as P

HI = lax.Precision.HIGHEST
F32 = jnp.float32
BF16 = jnp.bfloat16
B = 128
SB = 32
H = 64
PAYLOAD = 160
VMEM = pl.BlockSpec(memory_space=pltpu.VMEM)
HBM = pl.BlockSpec(memory_space=pltpu.HBM)
SMEM = pl.BlockSpec(memory_space=pltpu.SMEM)


def dot_tn(a, b, precision=HI):
    return lax.dot_general(a, b, (((0,), (0,)), ((), ())), precision=precision, preferred_element_type=F32)


def dot_nn(a, b, precision=HI):
    return lax.dot_general(a, b, (((1,), (0,)), ((), ())), precision=precision, preferred_element_type=F32)


def dot_nt(a, b, precision=HI):
    return lax.dot_general(a, b, (((1,), (1,)), ((), ())), precision=precision, preferred_element_type=F32)


def params(flops, mib=60):
    return dict(
        compiler_params=pltpu.CompilerParams(vmem_limit_bytes=mib * 2**20),
        cost_estimate=pl.CostEstimate(flops=flops, bytes_accessed=2**23, transcendentals=0),
    )


def pack_kernel(idx_ref, p_ref, o_ref):
    row, col = idx_ref[0], idx_ref[1]
    copies = o_ref.shape[0]

    def put(lo, value):
        for q in range(copies):
            o_ref[q, lo : lo + value.shape[0], 0 : value.shape[1]] = value

    for half in range(2):
        block = p_ref[:, half * B : half * B + B]
        other = 2 * col + half

        @pl.when(row <= other)
        def _():
            put(half * H, block[0:H, :])

        @pl.when(row > other)
        def _():
            put(half * H, block[:, H:B].T)

        @pl.when(row == other)
        def _():
            corner = block[H:B, H:B]
            put(2 * H, jnp.concatenate([corner[0:32], corner[32:64]], axis=1))


def unpack(src, parity, u_ref, nrow, ncol):
    for x in range(nrow // 2):
        i = 2 * x + parity
        for y in range(ncol):
            c = x * ncol + y
            for half in range(2):
                o = 2 * y + half
                piece = src[c, half * H : half * H + H, :]
                if i <= o:
                    u_ref[i * B : i * B + H, o * B : o * B + B] = piece
                else:
                    u_ref[o * B + H : o * B + B, i * B : i * B + B] = piece
                if i == o:
                    corner = src[c, 2 * H : 2 * H + 32, :]
                    low = jnp.concatenate([corner[:, 0:H], corner[:, H:B]], axis=0)
                    u_ref[i * B + H : i * B + B, i * B : i * B + B] = jnp.concatenate(
                        [piece[:, H:B].T, low], axis=1
                    )


def spread_row(value, r):
    return jnp.broadcast_to(value[r : r + 1, :], (8, B))


def chain(s_ref, s):
    nb, r0 = SB // 8, s * SB
    rowid = lax.broadcasted_iota(jnp.int32, (8, B), 0)
    blk = [s_ref[r0 + 8 * b : r0 + 8 * b + 8, 0:B] for b in range(nb)]
    c = [
        [
            jnp.broadcast_to(blk[b][:, r0 + i : r0 + i + 1], (8, B)) if b >= i // 8 else None
            for b in range(nb)
        ]
        for i in range(SB)
    ]
    x = [[s_ref[r0 + 8 * b : r0 + 8 * b + 8, B * h : B * h + B] for h in range(2)] for b in range(nb)]
    pivots = [None] * nb
    for j in range(SB):
        bj, rj = j // 8, j % 8
        p = spread_row(c[j][bj], rj)
        inv = 1.0 / p
        pivots[bj] = p if pivots[bj] is None else jnp.where(rowid == rj, p, pivots[bj])
        for i in range(j + 1, SB):
            m = spread_row(c[j][i // 8], i % 8) * inv
            for b in range(i // 8, nb):
                c[i][b] = c[i][b] - c[j][b] * m
        for h in range(2):
            xr = spread_row(x[bj][h], rj) * inv
            for b in range(bj, nb):
                cm = c[j][b] if b > bj else jnp.where(rowid > rj, c[j][b], 0.0)
                x[b][h] = x[b][h] - cm * xr
    out = []
    for b in range(nb):
        q = lax.rsqrt(pivots[b])
        out.append(jnp.concatenate([x[b][0] * q, x[b][1] * q], axis=1))
    return jnp.concatenate(out, axis=0)


def factor_block(s_ref):
    for s in range(B // SB):
        p = chain(s_ref, s)
        s_ref[SB * s : SB * s + SB, :] = p
        lo = SB * (s + 1)
        if lo < B:
            s_ref[lo:, :] = s_ref[lo:, :] - dot_tn(p[:, lo:B], p)


def chol_steps(u_ref, w_ref, s_ref, steps):
    n = u_ref.shape[1]
    ri = lax.broadcasted_iota(jnp.int32, (B, B), 0)
    ci = lax.broadcasted_iota(jnp.int32, (B, B), 1)
    eye = (ri == ci).astype(F32)

    def body(k, _):
        r0 = pl.multiple_of(k * B, B)
        s_ref[:, 0:B] = u_ref[pl.ds(r0, B), pl.ds(r0, B)]
        s_ref[:, B : 2 * B] = eye
        factor_block(s_ref)
        w = s_ref[:, B : 2 * B]
        for kk in range(steps):

            @pl.when(k == kk)
            def _():
                lo = (kk + 1) * B
                u_ref[kk * B : lo, kk * B : lo] = jnp.where(ri <= ci, s_ref[:, 0:B], 0.0)
                pair = kk // 2
                if kk % 2 == 0:
                    w_ref[pair, 0:B, 0:B] = w
                    w_ref[pair, 0:B, B : 2 * B] = jnp.zeros((B, B), F32)
                else:
                    w_ref[pair, B : 2 * B, B : 2 * B] = w
                    cross = dot_tn(u_ref[(kk - 1) * B : kk * B, kk * B : lo], w_ref[pair, 0:B, 0:B])
                    w_ref[pair, B : 2 * B, 0:B] = -dot_nn(w, cross)
                if lo < n:
                    panel = dot_nn(w, u_ref[kk * B : lo, lo:])
                    u_ref[kk * B : lo, lo:] = panel
                    t = lo
                    while t < n:
                        m = min(256, n - t)
                        u_ref[t : t + m, t:] = u_ref[t : t + m, t:] - dot_tn(
                            panel[:, t - lo : t - lo + m], panel[:, t - lo :]
                        )
                        t += m

        return 0

    lax.fori_loop(0, steps, body, 0)


def lower_block(u_ref, l_ref, row, first_col, col):
    rows, cols = l_ref.shape
    start = pl.multiple_of((col - first_col) * cols, B)
    part = u_ref[pl.ds(start, cols), pl.ds(pl.multiple_of(row * rows - first_col * cols, B), rows)].T
    rl = lax.broadcasted_iota(jnp.int32, (rows, cols), 0) + row * rows
    cl = lax.broadcasted_iota(jnp.int32, (rows, cols), 1) + col * cols
    l_ref[...] = jnp.where(rl >= cl, part, 0.0)


def copy_all(sources, targets, sems):
    copies = [pltpu.make_async_copy(s, t, sems.at[i]) for i, (s, t) in enumerate(zip(sources, targets))]
    for copy in copies:
        copy.start()
    return copies


def chol_first(idx_ref, mine_ref, other_ref, top_ref, rest_ref, w_ref, l_ref, u_ref, v_ref, s_ref, sems):
    row, col, core = idx_ref[0], idx_ref[1], idx_ref[2]
    nblk = u_ref.shape[0] // B
    ncol = mine_ref.shape[0] // (nblk // 2)
    for parity in range(2):

        @pl.when(core == parity)
        def _():
            unpack(mine_ref, parity, u_ref, nblk, ncol)
            unpack(other_ref, 1 - parity, u_ref, nblk, ncol)

    done = top_ref.shape[0]
    left = u_ref.shape[0] - done
    chol_steps(u_ref, v_ref, s_ref, done // B)
    sources = (u_ref.at[pl.ds(done, left), pl.ds(done, left)], u_ref.at[pl.ds(0, done)], v_ref)
    copies = copy_all(sources, (rest_ref, top_ref, w_ref), sems)

    @pl.when(col < w_ref.shape[0])
    def _():
        lower_block(u_ref, l_ref, row, 0, col)

    for copy in copies:
        copy.wait()


def chol_last(idx_ref, rest_ref, before_ref, last_ref, w_ref, l_ref, u_ref, v_ref, s_ref, sems):
    row, col, ncol = idx_ref[0], idx_ref[1], idx_ref[4]
    copy_all((rest_ref,), (u_ref,), sems)[0].wait()
    chol_steps(u_ref, v_ref, s_ref, u_ref.shape[0] // B)
    copies = copy_all((u_ref, v_ref), (last_ref, w_ref), sems)
    rows, cols = l_ref.shape
    first_col = ncol - u_ref.shape[0] // cols
    l_ref[...] = jnp.where(col < first_col, before_ref[...], 0.0)

    @pl.when((col >= first_col) & (row * rows >= first_col * cols))
    def _():
        lower_block(u_ref, l_ref, row, first_col, col)

    for copy in copies:
        copy.wait()


def split3(value):
    first = value.astype(BF16)
    rest = value - first.astype(F32)
    second = rest.astype(BF16)
    third = (rest - second.astype(F32)).astype(BF16)
    return first, second, third


def pick_rows(onehot, parts):
    return sum(dot_nn(onehot, part, None) for part in reversed(parts))


def pick_cols(parts, onehot):
    return sum(dot_nt(part, onehot, None) for part in reversed(parts))


def split2(value):
    first = value.astype(BF16)
    return first, (value - first.astype(F32)).astype(BF16)


def dot3(dot, a, b):
    return dot(a[0], b[1], None) + dot(a[1], b[0], None) + dot(a[0], b[0], None)


def solve_kernel(
    idx_ref, own_ref, mine_ref, other_ref, top_ref, last_ref, w0_ref, w1_ref, upd_ref, map_ref,
    fb_ref, schur_ref, send_ref,
    x_ref, u0_ref, u1_ref, v_ref, fh_ref, fl_ref, t_ref, o_ref, sem, sems,
):
    row, col, core, side = idx_ref[0], idx_ref[1], idx_ref[2], idx_ref[3]
    ncol, rows, width = own_ref.shape
    early = w0_ref.shape[0]

    def load(y):
        cols = pl.ds(y * width, width)
        found = [pltpu.make_async_copy(own_ref.at[y], x_ref.at[pl.ds(0, rows), cols], sem.at[y, 0])]
        for c, ref in ((core, mine_ref), (1 - core, other_ref)):
            target = pl.ds(pl.multiple_of((1 + c) * rows, B), rows)
            which = 1 if ref is mine_ref else 2
            found.append(pltpu.make_async_copy(ref.at[y], x_ref.at[target, cols], sem.at[y, which]))
        if y < early:
            tall = pl.ds(y * width, width)
            found.append(pltpu.make_async_copy(top_ref.at[tall], u0_ref.at[tall], sem.at[y, 3]))
            found.append(pltpu.make_async_copy(w0_ref.at[y], v_ref.at[y], sem.at[y, 4]))
        else:
            tall = pl.ds((y - early) * width, width)
            found.append(pltpu.make_async_copy(last_ref.at[tall], u1_ref.at[tall], sem.at[y, 3]))
            found.append(pltpu.make_async_copy(w1_ref.at[y - early], v_ref.at[y], sem.at[y, 4]))
        for copy in found:
            copy.start()
        return found

    waiting = [load(y) for y in range(ncol)]
    trailing = pltpu.make_async_copy(upd_ref, t_ref, sems.at[0])
    trailing.start()
    cut = u0_ref.shape[0]
    for k in range(ncol):
        for copy in waiting[k]:
            copy.wait()
        lo, hi = k * width, (k + 1) * width
        x = x_ref[:, lo:hi]
        if k > 0:
            top = min(lo, cut)
            x = x - dot3(dot_nn, (fh_ref[:, 0:top], fl_ref[:, 0:top]), split2(u0_ref[0:top, lo:hi]))
            if lo > cut:
                above = split2(u1_ref[0 : lo - cut, lo - cut : hi - cut])
                x = x - dot3(dot_nn, (fh_ref[:, cut:lo], fl_ref[:, cut:lo]), above)
        f = dot3(dot_nt, split2(x), split2(v_ref[k]))
        fh_ref[:, lo:hi], fl_ref[:, lo:hi] = split2(f)

        @pl.when(col == k)
        def _():
            fb_ref[...] = f[0:rows]

    trailing.wait()
    schur = t_ref[...] - dot3(
        dot_nt, (fh_ref[0:rows, :], fl_ref[0:rows, :]), (fh_ref[rows:, :], fl_ref[rows:, :])
    )
    t_ref[...] = schur
    out = pltpu.make_async_copy(t_ref, schur_ref, sems.at[1])
    out.start()
    half = o_ref.shape[0]
    place = lax.broadcasted_iota(jnp.int32, (half, rows), 0) + (row * 2 + 1 - side) * half
    onehot = (place == map_ref[...]).astype(F32).astype(BF16)
    o_ref[...] = pick_rows(onehot, split3(schur))
    sent = pltpu.make_async_copy(o_ref, send_ref, sems.at[2])
    sent.start()
    out.wait()
    sent.wait()


def widen(value, map_ref, first, base):
    blocks, rows = map_ref.shape
    width = value.shape[1] // blocks
    total = first.shape[1]
    step = total // blocks
    for b in range(blocks):
        lo = b * step // B * B
        hi = -((-(b + 1) * step) // B) * B
        place = lax.broadcasted_iota(jnp.int32, (hi - lo, width), 0) + (lo + base)
        onehot = (place == map_ref[b : b + 1, :]).astype(F32).astype(BF16)
        first[:, lo:hi] = first[:, lo:hi] + pick_cols(split3(value[:, b * width : (b + 1) * width]), onehot)


def own_kernel(idx_ref, schur_ref, row_map_ref, map_ref, diag_ref, o_ref):
    row, col, side = idx_ref[0], idx_ref[1], idx_ref[3]
    half, total = o_ref.shape
    rid = lax.broadcasted_iota(jnp.int32, (half, total), 0) + (row * 2 + side) * half
    cid = lax.broadcasted_iota(jnp.int32, (half, total), 1) + col * total
    o_ref[...] = jnp.where(rid == cid, diag_ref[...], 0.0)
    place = lax.broadcasted_iota(jnp.int32, (half, schur_ref.shape[0]), 0) + (row * 2 + side) * half
    onehot = (place == row_map_ref[...]).astype(F32).astype(BF16)
    widen(pick_rows(onehot, split3(schur_ref[...])), map_ref, o_ref, col * total)


def add_kernel(idx_ref, got_ref, map_ref, base_ref, o_ref):
    o_ref[...] = base_ref[...]
    widen(got_ref[...], map_ref, o_ref, idx_ref[1] * o_ref.shape[1])


def on_device(pivot, border, update, child_map, parent_diag):
    nrow, ncol = lax.axis_size("row"), lax.axis_size("col")
    row, col, leaf = lax.axis_index("row"), lax.axis_index("col"), lax.axis_index("leaf")
    nx = nrow // 2
    core, side = row % 2, leaf % 2
    idx = jnp.stack([row, col, core, side, jnp.int32(ncol)]).astype(jnp.int32)
    piece_rows, piece_cols = pivot.shape[1:]
    n = piece_rows * nrow
    rows, width = border.shape[1:]
    half = parent_diag.shape[1]
    total = 2 * half * nrow // ncol
    upd_cols = update.shape[2]

    chips = nx * ncol
    packed = pl.pallas_call(
        pack_kernel,
        out_shape=jax.ShapeDtypeStruct((chips, PAYLOAD, B), F32),
        in_specs=[SMEM, VMEM],
        out_specs=VMEM,
        **params(10**6),
    )(idx, pivot[0])
    groups = [[(2 * x + c) * ncol + y for x in range(nx) for y in range(ncol)] for c in range(2)]
    mine = lax.all_to_all(packed, ("row", "col"), 0, 0, axis_index_groups=groups, tiled=True)
    swap = [(r, r ^ 1) for r in range(nrow)]

    turn = [((2 * x + c) * ncol + y, (2 * y + c) * ncol + x) for x in range(nx) for c in range(2) for y in range(ncol)]
    turned = lax.ppermute(border[0], ("row", "col"), turn)
    turned, mine = lax.optimization_barrier((turned, mine))
    other = lax.ppermute(mine, "row", swap)
    same = [[2 * x + c for x in range(nx)] for c in range(2)]
    col_mine = lax.all_to_all(
        jnp.broadcast_to(turned, (nx, rows, width)), "row", 0, 0, axis_index_groups=same, tiled=True
    )

    pairs = n // (2 * B)
    early = 2
    inv = lambda count: jax.ShapeDtypeStruct((count, 2 * B, 2 * B), F32)
    done = early * 2 * B
    block = jax.ShapeDtypeStruct((piece_rows, piece_cols), F32)
    top, rest, inv0, begun = pl.pallas_call(
        chol_first,
        out_shape=(
            jax.ShapeDtypeStruct((done, n), F32),
            jax.ShapeDtypeStruct((n - done, n - done), F32),
            inv(early),
            block,
        ),
        in_specs=[SMEM, VMEM, VMEM],
        out_specs=(HBM, HBM, HBM, VMEM),
        scratch_shapes=[
            pltpu.VMEM((n, n), F32),
            pltpu.VMEM((early, 2 * B, 2 * B), F32),
            pltpu.VMEM((B, 2 * B), F32),
            pltpu.SemaphoreType.DMA((3,)),
        ],
        **params(10**10),
    )(idx, mine, other)

    bord, col_mine, inv0 = lax.optimization_barrier((border[0], col_mine, inv0))
    col_other = lax.ppermute(col_mine, "row", swap)
    own_rows = lax.all_to_all(jnp.broadcast_to(bord, (ncol, rows, width)), "col", 0, 0, tiled=True)

    last, inv1, pivot_out = pl.pallas_call(
        chol_last,
        out_shape=(jax.ShapeDtypeStruct((n - done, n - done), F32), inv(pairs - early), block),
        in_specs=[SMEM, HBM, VMEM],
        out_specs=(HBM, HBM, VMEM),
        scratch_shapes=[
            pltpu.VMEM((n - done, n - done), F32),
            pltpu.VMEM((pairs - early, 2 * B, 2 * B), F32),
            pltpu.VMEM((B, 2 * B), F32),
            pltpu.SemaphoreType.DMA((2,)),
        ],
        **params(3 * 10**10),
    )(idx, rest, begun)

    maps = lax.dynamic_slice(child_map, (leaf, row * rows), (1, rows))
    border_out, schur, send = pl.pallas_call(
        solve_kernel,
        out_shape=(
            jax.ShapeDtypeStruct((rows, width), F32),
            jax.ShapeDtypeStruct((rows, upd_cols), F32),
            jax.ShapeDtypeStruct((half, upd_cols), F32),
        ),
        in_specs=[SMEM] + [HBM] * 8 + [VMEM],
        out_specs=(VMEM, HBM, HBM),
        scratch_shapes=[
            pltpu.VMEM((3 * rows, n), F32),
            pltpu.VMEM((done, n), F32),
            pltpu.VMEM((n - done, n - done), F32),
            pltpu.VMEM((pairs, 2 * B, 2 * B), F32),
            pltpu.VMEM((3 * rows, n), BF16),
            pltpu.VMEM((3 * rows, n), BF16),
            pltpu.VMEM((rows, upd_cols), F32),
            pltpu.VMEM((half, upd_cols), F32),
            pltpu.SemaphoreType.DMA((ncol, 5)),
            pltpu.SemaphoreType.DMA((3,)),
        ],
        **params(10**10),
    )(idx, own_rows, col_mine, col_other, top, last, inv0, inv1, update[0], maps)

    got = lax.ppermute(send, "leaf", [(s, s ^ 1) for s in range(lax.axis_size("leaf"))])
    blocks = upd_cols // rows

    def col_maps(which):
        return lax.dynamic_slice(child_map, (which, col * upd_cols), (1, upd_cols)).reshape(blocks, rows)

    base = pl.pallas_call(
        own_kernel,
        out_shape=jax.ShapeDtypeStruct((half, total), F32),
        in_specs=[SMEM] + [VMEM] * 4,
        out_specs=VMEM,
        **params(2 * 10**9, 16),
    )(idx, schur, maps, col_maps(leaf), parent_diag.reshape(half, 1))
    parent_out = pl.pallas_call(
        add_kernel,
        out_shape=jax.ShapeDtypeStruct((half, total), F32),
        in_specs=[SMEM] + [VMEM] * 3,
        out_specs=VMEM,
        **params(2 * 10**9, 16),
    )(idx, got, col_maps(leaf ^ 1), base)
    return pivot_out[None], border_out[None], parent_out[None]


def solution(mesh):
    placed = (
        P("leaf", "row", "col"),
        P("leaf", "row", "col"),
        P("leaf", "row", "col"),
        P(),
        P("leaf", "row"),
    )
    return jax.shard_map(
        on_device,
        mesh=mesh,
        in_specs=placed,
        out_specs=(P("leaf", "row", "col"), P("leaf", "row", "col"), P("leaf", "row", "col")),
        check_vma=False,
    )
```

```python
import functools

import jax
import jax.numpy as jnp
from jax import lax
from jax.experimental import pallas as pl
from jax.experimental.pallas import tpu as pltpu
from jax.sharding import PartitionSpec as P

HI = lax.Precision.HIGHEST
F32 = jnp.float32
BF16 = jnp.bfloat16
B = 128
SB = 32
H = 64
PAYLOAD = 144
VMEM = pl.BlockSpec(memory_space=pltpu.VMEM)
HBM = pl.BlockSpec(memory_space=pltpu.HBM)
SMEM = pl.BlockSpec(memory_space=pltpu.SMEM)


def dot_tn(a, b, precision=HI):
    return lax.dot_general(a, b, (((0,), (0,)), ((), ())), precision=precision, preferred_element_type=F32)


def dot_nn(a, b, precision=HI):
    return lax.dot_general(a, b, (((1,), (0,)), ((), ())), precision=precision, preferred_element_type=F32)


def dot_nt(a, b, precision=HI):
    return lax.dot_general(a, b, (((1,), (1,)), ((), ())), precision=precision, preferred_element_type=F32)


def params(flops, mib=60):
    return dict(
        compiler_params=pltpu.CompilerParams(vmem_limit_bytes=mib * 2**20),
        cost_estimate=pl.CostEstimate(flops=flops, bytes_accessed=2**23, transcendentals=0),
    )


def pack_kernel(idx_ref, p_ref, o_ref):
    row, col = idx_ref[0], idx_ref[1]
    copies = o_ref.shape[0]

    def put(lo, value):
        for q in range(copies):
            o_ref[q, lo : lo + value.shape[0], :] = value

    for half in range(2):
        block = p_ref[:, half * B : half * B + B]
        other = 2 * col + half

        @pl.when(row < other)
        def _():
            put(half * H, block[0:H, :])

        @pl.when(row > other)
        def _():
            put(half * H, block[:, H:B].T)

        @pl.when(row == other)
        def _():
            q = H // 2
            put(half * H, block[0:q, :])
            put(half * H + q, jnp.concatenate([block[H : H + q, H : H + q], block[q:H, q:B]], axis=1))
            side = jnp.concatenate([block[H : H + q, H + q : B], block[H + q : B, H + q : B]], axis=1)
            put(2 * H, jnp.concatenate([side[0 : q // 2], side[q // 2 : q]], axis=1))


def unpack(src, parity, u_ref, nrow, ncol):
    for x in range(nrow // 2):
        i = 2 * x + parity
        for y in range(ncol):
            c = x * ncol + y
            for half in range(2):
                o = 2 * y + half
                piece = src[c, half * H : half * H + H, :]
                if i < o:
                    u_ref[i * B : i * B + H, o * B : o * B + B] = piece
                elif i > o:
                    u_ref[o * B + H : o * B + B, i * B : i * B + B] = piece
                else:
                    q = H // 2
                    u_ref[i * B : i * B + q, i * B : i * B + B] = piece[0:q]
                    u_ref[i * B + q : i * B + H, i * B : i * B + B] = jnp.concatenate(
                        [piece[0:q, q:H].T, piece[q:H, q:B]], axis=1
                    )
                    side = src[c, 2 * H : 2 * H + q // 2, :]
                    side = jnp.concatenate([side[:, 0:H], side[:, H:B]], axis=0)
                    right = jnp.concatenate(
                        [
                            jnp.concatenate([piece[q:H, 0:q], side[:, 0:q]], axis=1),
                            jnp.concatenate([side[:, 0:q].T, side[:, q:H]], axis=1),
                        ],
                        axis=0,
                    )
                    cross = jnp.concatenate([piece[0:q, H:B], piece[q:H, H:B]], axis=0).T
                    u_ref[i * B + H : i * B + B, i * B : i * B + B] = jnp.concatenate([cross, right], axis=1)


def spread_row(value, r):
    return jnp.broadcast_to(value[r : r + 1, :], (8, B))


def chain(s_ref, s):
    nb, r0 = SB // 8, s * SB
    rowid = lax.broadcasted_iota(jnp.int32, (8, B), 0)
    blk = [s_ref[r0 + 8 * b : r0 + 8 * b + 8, 0:B] for b in range(nb)]
    c = [
        [
            jnp.broadcast_to(blk[b][:, r0 + i : r0 + i + 1], (8, B)) if b >= i // 8 else None
            for b in range(nb)
        ]
        for i in range(SB)
    ]
    x = [[s_ref[r0 + 8 * b : r0 + 8 * b + 8, B * h : B * h + B] for h in range(2)] for b in range(nb)]
    pivots = [None] * nb
    for j in range(SB):
        bj, rj = j // 8, j % 8
        p = spread_row(c[j][bj], rj)
        inv = 1.0 / p
        pivots[bj] = p if pivots[bj] is None else jnp.where(rowid == rj, p, pivots[bj])
        for i in range(j + 1, SB):
            m = spread_row(c[j][i // 8], i % 8) * inv
            for b in range(i // 8, nb):
                c[i][b] = c[i][b] - c[j][b] * m
        for h in range(2):
            xr = spread_row(x[bj][h], rj) * inv
            for b in range(bj, nb):
                cm = c[j][b] if b > bj else jnp.where(rowid > rj, c[j][b], 0.0)
                x[b][h] = x[b][h] - cm * xr
    out = []
    for b in range(nb):
        q = lax.rsqrt(pivots[b])
        out.append(jnp.concatenate([x[b][0] * q, x[b][1] * q], axis=1))
    return jnp.concatenate(out, axis=0)


def factor_block(s_ref):
    for q in range(B // SB):
        p = chain(s_ref, q)
        s_ref[SB * q : SB * q + SB, :] = p
        below = SB * (q + 1)
        if below < B:
            s_ref[below:, :] = s_ref[below:, :] - dot_tn(p[:, below:B], p)


def chol_steps(u_ref, w_ref, s_ref, steps):
    n = u_ref.shape[0]
    ri = lax.broadcasted_iota(jnp.int32, (B, B), 0)
    ci = lax.broadcasted_iota(jnp.int32, (B, B), 1)
    eye = (ri == ci).astype(F32)

    def body(k, _):
        r0 = pl.multiple_of(k * B, B)
        s_ref[:, 0:B] = u_ref[pl.ds(r0, B), pl.ds(r0, B)]
        s_ref[:, B : 2 * B] = eye
        factor_block(s_ref)
        w = s_ref[:, B : 2 * B]
        for kk in range(steps):

            @pl.when(k == kk)
            def _():
                lo = (kk + 1) * B
                u_ref[kk * B : lo, kk * B : lo] = jnp.where(ri <= ci, s_ref[:, 0:B], 0.0)
                place = slice(kk % 2 * B, kk % 2 * B + B)
                w_ref[kk // 2, place, place] = w
                if lo < n:
                    panel = dot_nn(w, u_ref[kk * B : lo, lo:])
                    u_ref[kk * B : lo, lo:] = panel
                    for t in range(lo, n, 2 * B):
                        m = min(2 * B, n - t)
                        u_ref[t : t + m, t:] = u_ref[t : t + m, t:] - dot_tn(
                            panel[:, t - lo : t - lo + m], panel[:, t - lo :]
                        )

        return 0

    lax.fori_loop(0, steps, body, 0)
    for pair in range(steps // 2):
        lo = 2 * pair * B
        cross = dot_tn(u_ref[lo : lo + B, lo + B : lo + 2 * B], w_ref[pair, 0:B, 0:B])
        w_ref[pair, B : 2 * B, 0:B] = -dot_nn(w_ref[pair, B : 2 * B, B : 2 * B], cross)
        w_ref[pair, 0:B, B : 2 * B] = jnp.zeros((B, B), F32)


def lower_block(u_ref, l_ref, row, first_col, col):
    rows, cols = l_ref.shape
    start = pl.multiple_of((col - first_col) * cols, B)
    part = u_ref[pl.ds(start, cols), pl.ds(pl.multiple_of(row * rows - first_col * cols, B), rows)].T
    rl = lax.broadcasted_iota(jnp.int32, (rows, cols), 0) + row * rows
    cl = lax.broadcasted_iota(jnp.int32, (rows, cols), 1) + col * cols
    l_ref[...] = jnp.where(rl >= cl, part, 0.0)


def copy_all(sources, targets, sems):
    copies = [pltpu.make_async_copy(s, t, sems.at[i]) for i, (s, t) in enumerate(zip(sources, targets))]
    for copy in copies:
        copy.start()
    return copies


def chol_first(idx_ref, mine_ref, other_ref, top_ref, rest_ref, w_ref, l_ref, u_ref, v_ref, s_ref, sems):
    row, col, core = idx_ref[0], idx_ref[1], idx_ref[2]
    nblk = u_ref.shape[0] // B
    ncol = mine_ref.shape[0] // (nblk // 2)
    for parity in range(2):

        @pl.when(core == parity)
        def _():
            unpack(mine_ref, parity, u_ref, nblk, ncol)
            unpack(other_ref, 1 - parity, u_ref, nblk, ncol)

    chol_end(u_ref, v_ref, s_ref, sems, top_ref, rest_ref, w_ref, l_ref, row, col, 0)


def chol_next(first_col, idx_ref, from_ref, before_ref, *refs):
    if len(refs) == 8:
        top_ref, rest_ref, w_ref, l_ref, u_ref, v_ref, s_ref, sems = refs
    else:
        w_ref, l_ref, u_ref, v_ref, s_ref, sems = refs
        top_ref = rest_ref = None
    copy_all((from_ref,), (u_ref,), sems)[0].wait()
    l_ref[...] = before_ref[...]
    chol_end(u_ref, v_ref, s_ref, sems, top_ref, rest_ref, w_ref, l_ref, idx_ref[0], idx_ref[1], first_col)


def chol_end(u_ref, v_ref, s_ref, sems, top_ref, rest_ref, w_ref, l_ref, row, col, first_col):
    count = w_ref.shape[0]
    done = count * 2 * B
    left = u_ref.shape[0] - done
    chol_steps(u_ref, v_ref, s_ref, count * 2)
    sources, targets = (v_ref,), (w_ref,)
    if left > 0:
        sources += (u_ref.at[pl.ds(done, left), pl.ds(done, left)], u_ref.at[pl.ds(0, done)])
        targets += (rest_ref, top_ref)
    copies = copy_all(sources, targets, sems)
    rows, cols = l_ref.shape
    if first_col == 0:
        l_ref[...] = jnp.zeros_like(l_ref)

    @pl.when((col >= first_col) & (col < first_col + count) & (row * rows >= first_col * cols))
    def _():
        lower_block(u_ref, l_ref, row, first_col, col)

    for copy in copies:
        copy.wait()


def split3(value):
    first = value.astype(BF16)
    rest = value - first.astype(F32)
    second = rest.astype(BF16)
    third = (rest - second.astype(F32)).astype(BF16)
    return first, second, third


def pick_rows(onehot, parts):
    return sum(dot_nn(onehot, part, None) for part in reversed(parts))


def pick_cols(parts, onehot):
    return sum(dot_nt(part, onehot, None) for part in reversed(parts))


def split2(value):
    first = value.astype(BF16)
    return first, (value - first.astype(F32)).astype(BF16)


def dot3(dot, a, b):
    return dot(a[0], b[1], None) + dot(a[1], b[0], None) + dot(a[0], b[0], None)


def solve_kernel(
    idx_ref, own_ref, mine_ref, other_ref, top0_ref, top1_ref,
    w0_ref, w1_ref, w2_ref, upd_ref, map_ref,
    fb_ref, schur_ref, send_ref,
    x_ref, u0_ref, u1_ref, v_ref, fh_ref, fl_ref, t_ref, o_ref, sem, sems,
):
    row, col, core, side, leaf = idx_ref[0], idx_ref[1], idx_ref[2], idx_ref[3], idx_ref[5]
    ncol, rows, width = mine_ref.shape

    def load(y):
        cols = pl.ds(y * width, width)
        found = [pltpu.make_async_copy(own_ref.at[y], x_ref.at[pl.ds(0, rows), cols], sem.at[y, 0])]
        for c, ref in ((core, mine_ref), (1 - core, other_ref)):
            target = pl.ds(pl.multiple_of((1 + c) * rows, B), rows)
            which = 1 if ref is mine_ref else 2
            found.append(pltpu.make_async_copy(ref.at[y], x_ref.at[target, cols], sem.at[y, which]))
        inverse = (w0_ref.at[0], w1_ref.at[0], w1_ref.at[1], w2_ref.at[0])[y]
        found.append(pltpu.make_async_copy(inverse, v_ref.at[y], sem.at[y, 3]))
        if y == 0:
            found.append(pltpu.make_async_copy(top0_ref, u0_ref, sem.at[y, 4]))
        if y == 1:
            found.append(pltpu.make_async_copy(top1_ref, u1_ref, sem.at[y, 4]))
        for copy in found:
            copy.start()
        return found

    waiting = [load(y) for y in range(ncol)]
    trailing = pltpu.make_async_copy(upd_ref, t_ref, sems.at[0])
    trailing.start()
    cut = u0_ref.shape[0]
    for k in range(ncol):
        for copy in waiting[k]:
            copy.wait()
        lo, hi = k * width, (k + 1) * width
        x = x_ref[:, lo:hi]
        if k > 0:
            top = min(lo, cut)
            x = x - dot3(dot_nn, (fh_ref[:, 0:top], fl_ref[:, 0:top]), split2(u0_ref[0:top, lo:hi]))
            if lo > cut:
                above = split2(u1_ref[0 : lo - cut, lo - cut : hi - cut])
                x = x - dot3(dot_nn, (fh_ref[:, cut:lo], fl_ref[:, cut:lo]), above)
        f = dot3(dot_nt, split2(x), split2(v_ref[k]))
        fh_ref[:, lo:hi], fl_ref[:, lo:hi] = split2(f)

        @pl.when(col == k)
        def _():
            fb_ref[...] = f[0:rows]

    trailing.wait()
    schur = t_ref[...] - dot3(
        dot_nt, (fh_ref[0:rows, :], fl_ref[0:rows, :]), (fh_ref[rows:, :], fl_ref[rows:, :])
    )
    t_ref[...] = schur
    out = pltpu.make_async_copy(t_ref, schur_ref, sems.at[1])
    out.start()
    half = o_ref.shape[0]
    place = lax.broadcasted_iota(jnp.int32, (half, rows), 0) + (row * 2 + 1 - side) * half
    row_map = map_ref[pl.ds(leaf, 1), pl.ds(pl.multiple_of(row * rows, B), rows)]
    onehot = (place == row_map).astype(F32).astype(BF16)
    o_ref[...] = pick_rows(onehot, split3(schur))
    sent = pltpu.make_async_copy(o_ref, send_ref, sems.at[2])
    sent.start()
    out.wait()
    sent.wait()


def widen(value, maps, first, base):
    blocks = len(maps)
    width = value.shape[1] // blocks
    total = first.shape[1]
    step = total // blocks
    for b in range(blocks):
        lo = b * step // B * B
        hi = -((-(b + 1) * step) // B) * B
        place = lax.broadcasted_iota(jnp.int32, (hi - lo, width), 0) + (lo + base)
        onehot = (place == maps[b]).astype(F32).astype(BF16)
        first[:, lo:hi] = first[:, lo:hi] + pick_cols(split3(value[:, b * width : (b + 1) * width]), onehot)


def col_maps(map_ref, leaf, col, rows, cols):
    return [
        map_ref[pl.ds(leaf, 1), pl.ds(pl.multiple_of(col * cols + b * rows, B), rows)] for b in range(cols // rows)
    ]


def own_kernel(idx_ref, schur_ref, map_ref, diag_ref, o_ref):
    row, col, side, leaf = idx_ref[0], idx_ref[1], idx_ref[3], idx_ref[5]
    half, total = o_ref.shape
    rows, cols = schur_ref.shape
    rid = lax.broadcasted_iota(jnp.int32, (half, total), 0) + (row * 2 + side) * half
    cid = lax.broadcasted_iota(jnp.int32, (half, total), 1) + col * total
    o_ref[...] = jnp.where(rid == cid, diag_ref[...], 0.0)
    place = lax.broadcasted_iota(jnp.int32, (half, rows), 0) + (row * 2 + side) * half
    row_map = map_ref[pl.ds(leaf, 1), pl.ds(pl.multiple_of(row * rows, B), rows)]
    onehot = (place == row_map).astype(F32).astype(BF16)
    maps = col_maps(map_ref, leaf, col, rows, cols)
    widen(pick_rows(onehot, split3(schur_ref[...])), maps, o_ref, col * total)


def add_kernel(rows, idx_ref, got_ref, map_ref, base_ref, o_ref):
    side, leaf, col = idx_ref[3], idx_ref[5], idx_ref[1]
    o_ref[...] = base_ref[...]
    maps = col_maps(map_ref, leaf + 1 - 2 * side, col, rows, got_ref.shape[1])
    widen(got_ref[...], maps, o_ref, col * o_ref.shape[1])


def on_device(pivot, border, update, child_map, parent_diag):
    nrow, ncol = lax.axis_size("row"), lax.axis_size("col")
    row, col, leaf = lax.axis_index("row"), lax.axis_index("col"), lax.axis_index("leaf")
    nx = nrow // 2
    core, side = row % 2, leaf % 2
    idx = jnp.stack([row, col, core, side, jnp.int32(ncol), leaf]).astype(jnp.int32)
    piece_rows, piece_cols = pivot.shape[1:]
    n = piece_rows * nrow
    rows, width = border.shape[1:]
    half = parent_diag.shape[1]
    total = 2 * half * nrow // ncol
    upd_cols = update.shape[2]

    chips = nx * ncol
    packed = pl.pallas_call(
        pack_kernel,
        out_shape=jax.ShapeDtypeStruct((chips, PAYLOAD, B), F32),
        in_specs=[SMEM, VMEM],
        out_specs=VMEM,
        **params(10**6),
    )(idx, pivot[0])
    groups = [[(2 * x + c) * ncol + y for x in range(nx) for y in range(ncol)] for c in range(2)]
    mine = lax.all_to_all(packed, ("row", "col"), 0, 0, axis_index_groups=groups, tiled=True)
    swap = [(r, r ^ 1) for r in range(nrow)]

    turn = [((2 * x + c) * ncol + y, (2 * y + c) * ncol + x) for x in range(nx) for c in range(2) for y in range(ncol)]
    bord, mine = lax.optimization_barrier((border[0], mine))
    turned = lax.ppermute(bord, ("row", "col"), turn)
    other = lax.ppermute(mine, "row", swap)

    def factor(kernel, order, count, operands, specs, work):
        left = order - 2 * B * count
        square = lambda m: jax.ShapeDtypeStruct((m, m), F32)
        shapes = [square(left)] if left else []
        if left:
            shapes = [jax.ShapeDtypeStruct((2 * B * count, order), F32)] + shapes
        shapes += [
            jax.ShapeDtypeStruct((count, 2 * B, 2 * B), F32),
            jax.ShapeDtypeStruct((piece_rows, piece_cols), F32),
        ]
        return pl.pallas_call(
            kernel,
            out_shape=tuple(shapes),
            in_specs=[SMEM] + specs,
            out_specs=tuple([HBM] * (len(shapes) - 1) + [VMEM]),
            scratch_shapes=[
                pltpu.VMEM((order, order), F32),
                pltpu.VMEM((count, 2 * B, 2 * B), F32),
                pltpu.VMEM((B, 2 * B), F32),
                pltpu.SemaphoreType.DMA((3,)),
            ],
            **params(work, 58),
        )(idx, *operands)

    top0, rest, inv0, block = factor(chol_first, n, 1, (mine, other), [VMEM, VMEM], 10**10)

    bord, turned, inv0 = lax.optimization_barrier((bord, turned, inv0))
    same = [[2 * x + c for x in range(nx)] for c in range(2)]
    col_mine = lax.all_to_all(
        jnp.broadcast_to(turned, (nx, rows, width)), "row", 0, 0, axis_index_groups=same, tiled=True
    )

    middle = n // (2 * B) - 2
    top1, rest, inv1, block = factor(
        functools.partial(chol_next, 1), n - 2 * B, middle, (rest, block), [HBM, VMEM], 2 * 10**10
    )
    col_mine, rest, bord = lax.optimization_barrier((col_mine, rest, bord))
    col_other = lax.ppermute(col_mine, "row", swap)
    own = lax.all_to_all(jnp.broadcast_to(bord, (ncol, rows, width)), "col", 0, 0, tiled=True)
    inv2, pivot_out = factor(functools.partial(chol_next, 1 + middle), 2 * B, 1, (rest, block), [HBM, VMEM], 10**10)

    border_out, schur, send = pl.pallas_call(
        solve_kernel,
        out_shape=(
            jax.ShapeDtypeStruct((rows, width), F32),
            jax.ShapeDtypeStruct((rows, upd_cols), F32),
            jax.ShapeDtypeStruct((half, upd_cols), F32),
        ),
        in_specs=[SMEM] + [HBM] * 9 + [VMEM],
        out_specs=(VMEM, HBM, HBM),
        scratch_shapes=[
            pltpu.VMEM((3 * rows, n), F32),
            pltpu.VMEM(top0.shape, F32),
            pltpu.VMEM(top1.shape, F32),
            pltpu.VMEM((ncol, 2 * B, 2 * B), F32),
            pltpu.VMEM((3 * rows, n), BF16),
            pltpu.VMEM((3 * rows, n), BF16),
            pltpu.VMEM((rows, upd_cols), F32),
            pltpu.VMEM((half, upd_cols), F32),
            pltpu.SemaphoreType.DMA((ncol, 5)),
            pltpu.SemaphoreType.DMA((3,)),
        ],
        **params(10**10),
    )(idx, own, col_mine, col_other, top0, top1, inv0, inv1, inv2, update[0], child_map)

    got = lax.ppermute(send, "leaf", [(s, s ^ 1) for s in range(lax.axis_size("leaf"))])
    base = pl.pallas_call(
        own_kernel,
        out_shape=jax.ShapeDtypeStruct((half, total), F32),
        in_specs=[SMEM] + [VMEM] * 3,
        out_specs=VMEM,
        **params(2 * 10**9, 16),
    )(idx, schur, child_map, parent_diag.reshape(half, 1))
    parent_out = pl.pallas_call(
        functools.partial(add_kernel, rows),
        out_shape=jax.ShapeDtypeStruct((half, total), F32),
        in_specs=[SMEM] + [VMEM] * 3,
        out_specs=VMEM,
        **params(2 * 10**9, 16),
    )(idx, got, child_map, base)
    return pivot_out[None], border_out[None], parent_out[None]


def solution(mesh):
    placed = (
        P("leaf", "row", "col"),
        P("leaf", "row", "col"),
        P("leaf", "row", "col"),
        P(),
        P("leaf", "row"),
    )
    return jax.shard_map(
        on_device,
        mesh=mesh,
        in_specs=placed,
        out_specs=(P("leaf", "row", "col"), P("leaf", "row", "col"), P("leaf", "row", "col")),
        check_vma=False,
    )
```

```python
import functools

import jax
import jax.numpy as jnp
from jax import lax
from jax.experimental import pallas as pl
from jax.experimental.pallas import tpu as pltpu
from jax.sharding import PartitionSpec as P

HI = lax.Precision.HIGHEST
F32 = jnp.float32
BF16 = jnp.bfloat16
B = 128
SB = 32
H = 64
PAYLOAD = 144
VMEM = pl.BlockSpec(memory_space=pltpu.VMEM)
HBM = pl.BlockSpec(memory_space=pltpu.HBM)
SMEM = pl.BlockSpec(memory_space=pltpu.SMEM)


def dot_tn(a, b, precision=HI):
    return lax.dot_general(a, b, (((0,), (0,)), ((), ())), precision=precision, preferred_element_type=F32)


def dot_nn(a, b, precision=HI):
    return lax.dot_general(a, b, (((1,), (0,)), ((), ())), precision=precision, preferred_element_type=F32)


def dot_nt(a, b, precision=HI):
    return lax.dot_general(a, b, (((1,), (1,)), ((), ())), precision=precision, preferred_element_type=F32)


def params(flops, mib=60):
    return dict(
        compiler_params=pltpu.CompilerParams(vmem_limit_bytes=mib * 2**20),
        cost_estimate=pl.CostEstimate(flops=flops, bytes_accessed=2**23, transcendentals=0),
    )


def pack_kernel(idx_ref, p_ref, o_ref):
    row, col = idx_ref[0], idx_ref[1]
    copies = o_ref.shape[0]

    def put(lo, value):
        for q in range(copies):
            o_ref[q, lo : lo + value.shape[0], :] = value

    for half in range(2):
        block = p_ref[:, half * B : half * B + B]
        other = 2 * col + half

        @pl.when(row < other)
        def _():
            put(half * H, block[0:H, :])

        @pl.when(row > other)
        def _():
            put(half * H, block[:, H:B].T)

        @pl.when(row == other)
        def _():
            q = H // 2
            put(half * H, block[0:q, :])
            put(half * H + q, jnp.concatenate([block[H : H + q, H : H + q], block[q:H, q:B]], axis=1))
            side = jnp.concatenate([block[H : H + q, H + q : B], block[H + q : B, H + q : B]], axis=1)
            put(2 * H, jnp.concatenate([side[0 : q // 2], side[q // 2 : q]], axis=1))


def unpack(src, parity, u_ref, nrow, ncol):
    for x in range(nrow // 2):
        i = 2 * x + parity
        for y in range(ncol):
            c = x * ncol + y
            for half in range(2):
                o = 2 * y + half
                piece = src[c, half * H : half * H + H, :]
                if i < o:
                    u_ref[i * B : i * B + H, o * B : o * B + B] = piece
                elif i > o:
                    u_ref[o * B + H : o * B + B, i * B : i * B + B] = piece
                else:
                    q = H // 2
                    u_ref[i * B : i * B + q, i * B : i * B + B] = piece[0:q]
                    u_ref[i * B + q : i * B + H, i * B : i * B + B] = jnp.concatenate(
                        [piece[0:q, q:H].T, piece[q:H, q:B]], axis=1
                    )
                    side = src[c, 2 * H : 2 * H + q // 2, :]
                    side = jnp.concatenate([side[:, 0:H], side[:, H:B]], axis=0)
                    right = jnp.concatenate(
                        [
                            jnp.concatenate([piece[q:H, 0:q], side[:, 0:q]], axis=1),
                            jnp.concatenate([side[:, 0:q].T, side[:, q:H]], axis=1),
                        ],
                        axis=0,
                    )
                    cross = jnp.concatenate([piece[0:q, H:B], piece[q:H, H:B]], axis=0).T
                    u_ref[i * B + H : i * B + B, i * B : i * B + B] = jnp.concatenate([cross, right], axis=1)


def spread_row(value, r):
    return jnp.broadcast_to(value[r : r + 1, :], (8, B))


def chain(s_ref, s):
    nb, r0 = SB // 8, s * SB
    rowid = lax.broadcasted_iota(jnp.int32, (8, B), 0)
    blk = [s_ref[r0 + 8 * b : r0 + 8 * b + 8, 0:B] for b in range(nb)]
    c = [
        [
            jnp.broadcast_to(blk[b][:, r0 + i : r0 + i + 1], (8, B)) if b >= i // 8 else None
            for b in range(nb)
        ]
        for i in range(SB)
    ]
    x = [[s_ref[r0 + 8 * b : r0 + 8 * b + 8, B * h : B * h + B] for h in range(2)] for b in range(nb)]
    pivots = [None] * nb
    for j in range(SB):
        bj, rj = j // 8, j % 8
        p = spread_row(c[j][bj], rj)
        inv = 1.0 / p
        pivots[bj] = p if pivots[bj] is None else jnp.where(rowid == rj, p, pivots[bj])
        for i in range(j + 1, SB):
            m = spread_row(c[j][i // 8], i % 8) * inv
            for b in range(i // 8, nb):
                c[i][b] = c[i][b] - c[j][b] * m
        for h in range(2):
            xr = spread_row(x[bj][h], rj) * inv
            for b in range(bj, nb):
                cm = c[j][b] if b > bj else jnp.where(rowid > rj, c[j][b], 0.0)
                x[b][h] = x[b][h] - cm * xr
    out = []
    for b in range(nb):
        q = lax.rsqrt(pivots[b])
        out.append(jnp.concatenate([x[b][0] * q, x[b][1] * q], axis=1))
    return jnp.concatenate(out, axis=0)


def factor_block(s_ref):
    for q in range(B // SB):
        p = chain(s_ref, q)
        s_ref[SB * q : SB * q + SB, :] = p
        below = SB * (q + 1)
        if below < B:
            s_ref[below:, :] = s_ref[below:, :] - dot_tn(p[:, below:B], p)


def chol_steps(u_ref, w_ref, s_ref, steps):
    n = u_ref.shape[0]
    ri = lax.broadcasted_iota(jnp.int32, (B, B), 0)
    ci = lax.broadcasted_iota(jnp.int32, (B, B), 1)
    eye = (ri == ci).astype(F32)

    def body(k, _):
        r0 = pl.multiple_of(k * B, B)
        s_ref[:, 0:B] = u_ref[pl.ds(r0, B), pl.ds(r0, B)]
        s_ref[:, B : 2 * B] = eye
        factor_block(s_ref)
        w = s_ref[:, B : 2 * B]
        for kk in range(steps):

            @pl.when(k == kk)
            def _():
                lo = (kk + 1) * B
                u_ref[kk * B : lo, kk * B : lo] = jnp.where(ri <= ci, s_ref[:, 0:B], 0.0)
                place = slice(kk % 2 * B, kk % 2 * B + B)
                w_ref[kk // 2, place, place] = w
                if lo < n:
                    panel = dot_nn(w, u_ref[kk * B : lo, lo:])
                    u_ref[kk * B : lo, lo:] = panel
                    for t in range(lo, n, 2 * B):
                        m = min(2 * B, n - t)
                        u_ref[t : t + m, t:] = u_ref[t : t + m, t:] - dot_tn(
                            panel[:, t - lo : t - lo + m], panel[:, t - lo :]
                        )

        return 0

    lax.fori_loop(0, steps, body, 0)
    for pair in range(steps // 2):
        lo = 2 * pair * B
        cross = dot_tn(u_ref[lo : lo + B, lo + B : lo + 2 * B], w_ref[pair, 0:B, 0:B])
        w_ref[pair, B : 2 * B, 0:B] = -dot_nn(w_ref[pair, B : 2 * B, B : 2 * B], cross)
        w_ref[pair, 0:B, B : 2 * B] = jnp.zeros((B, B), F32)


def lower_block(u_ref, l_ref, row, first_col, col):
    rows, cols = l_ref.shape
    start = pl.multiple_of((col - first_col) * cols, B)
    part = u_ref[pl.ds(start, cols), pl.ds(pl.multiple_of(row * rows - first_col * cols, B), rows)].T
    rl = lax.broadcasted_iota(jnp.int32, (rows, cols), 0) + row * rows
    cl = lax.broadcasted_iota(jnp.int32, (rows, cols), 1) + col * cols
    l_ref[...] = jnp.where(rl >= cl, part, 0.0)


def copy_all(sources, targets, sems):
    copies = [pltpu.make_async_copy(s, t, sems.at[i]) for i, (s, t) in enumerate(zip(sources, targets))]
    for copy in copies:
        copy.start()
    return copies


def chol_first(idx_ref, mine_ref, other_ref, top_ref, rest_ref, w_ref, l_ref, u_ref, v_ref, s_ref, sems):
    row, col, core = idx_ref[0], idx_ref[1], idx_ref[2]
    nblk = u_ref.shape[0] // B
    ncol = mine_ref.shape[0] // (nblk // 2)
    for parity in range(2):

        @pl.when(core == parity)
        def _():
            unpack(mine_ref, parity, u_ref, nblk, ncol)
            unpack(other_ref, 1 - parity, u_ref, nblk, ncol)

    chol_end(u_ref, v_ref, s_ref, sems, top_ref, rest_ref, w_ref, l_ref, row, col, 0)


def chol_next(first_col, idx_ref, from_ref, before_ref, *refs):
    top_ref, w_ref, l_ref, u_ref, v_ref, s_ref, sems = refs
    copy_all((from_ref,), (u_ref,), sems)[0].wait()
    l_ref[...] = before_ref[...]
    chol_end(u_ref, v_ref, s_ref, sems, top_ref, None, w_ref, l_ref, idx_ref[0], idx_ref[1], first_col)


def chol_end(u_ref, v_ref, s_ref, sems, top_ref, rest_ref, w_ref, l_ref, row, col, first_col):
    count = w_ref.shape[0]
    done = count * 2 * B
    left = u_ref.shape[0] - done
    chol_steps(u_ref, v_ref, s_ref, count * 2)
    sources, targets = (v_ref, u_ref.at[pl.ds(0, done)]), (w_ref, top_ref)
    if left > 0:
        sources += (u_ref.at[pl.ds(done, left), pl.ds(done, left)],)
        targets += (rest_ref,)
    copies = copy_all(sources, targets, sems)
    rows, cols = l_ref.shape
    if first_col == 0:
        l_ref[...] = jnp.zeros_like(l_ref)

    @pl.when((col >= first_col) & (col < first_col + count) & (row * rows >= first_col * cols))
    def _():
        lower_block(u_ref, l_ref, row, first_col, col)

    for copy in copies:
        copy.wait()


def split3(value):
    first = value.astype(BF16)
    rest = value - first.astype(F32)
    second = rest.astype(BF16)
    third = (rest - second.astype(F32)).astype(BF16)
    return first, second, third


def pick_rows(onehot, parts):
    return sum(dot_nn(onehot, part, None) for part in reversed(parts))


def pick_cols(parts, onehot):
    return sum(dot_nt(part, onehot, None) for part in reversed(parts))


def split2(value):
    first = value.astype(BF16)
    return first, (value - first.astype(F32)).astype(BF16)


def dot3(dot, a, b):
    return dot(a[0], b[1], None) + dot(a[1], b[0], None) + dot(a[0], b[0], None)


def solve_rows(x_ref, fh_ref, fl_ref, u0_ref, u1_ref, v_ref, ready, done):
    cut = u0_ref.shape[0]
    count, width = v_ref.shape[:2]
    for k in range(count):
        ready(k)
        lo, hi = k * width, (k + 1) * width
        x = x_ref[:, lo:hi]
        if k > 0:
            top = min(lo, cut)
            x = x - dot3(dot_nn, (fh_ref[:, 0:top], fl_ref[:, 0:top]), split2(u0_ref[0:top, lo:hi]))
            if lo > cut:
                above = split2(u1_ref[0 : lo - cut, lo - cut : hi - cut])
                x = x - dot3(dot_nn, (fh_ref[:, cut:lo], fl_ref[:, cut:lo]), above)
        f = dot3(dot_nt, split2(x), split2(v_ref[k]))
        fh_ref[:, lo:hi], fl_ref[:, lo:hi] = split2(f)
        done(k, f)


def load_factor(y, top0_ref, top1_ref, w0_ref, w1_ref, u0_ref, u1_ref, v_ref, sem):
    early = w0_ref.shape[0]
    inverse = w0_ref.at[y] if y < early else w1_ref.at[y - early]
    found = [pltpu.make_async_copy(inverse, v_ref.at[y], sem.at[y, 0])]
    if y == 0:
        found.append(pltpu.make_async_copy(top0_ref, u0_ref, sem.at[y, 1]))
    if y == 1:
        found.append(pltpu.make_async_copy(top1_ref, u1_ref, sem.at[y, 1]))
    return found


def solve_first(
    idx_ref, own0_ref, own1_ref, own2_ref, own3_ref, mine_ref, top0_ref, top1_ref, w0_ref, w1_ref, upd_ref,
    fb_ref, oh_ref, ol_ref, part_ref,
    x_ref, u0_ref, u1_ref, v_ref, fh_ref, fl_ref, t_ref, sem, sems,
):
    col, core = idx_ref[1], idx_ref[2]
    ncol, rows, width = mine_ref.shape
    waiting = []
    for y in range(ncol):
        found = load_factor(y, top0_ref, top1_ref, w0_ref, w1_ref, u0_ref, u1_ref, v_ref, sem)
        cols = pl.ds(y * width, width)
        found.append(pltpu.make_async_copy(mine_ref.at[y], x_ref.at[pl.ds(rows, rows), cols], sem.at[y, 2]))
        if y == 0:
            for d, ref in enumerate((own0_ref, own1_ref, own2_ref, own3_ref)):
                whose = lax.rem(col + ncol - d, ncol)
                target = pl.ds(pl.multiple_of(whose * width, B), width)
                found.append(pltpu.make_async_copy(ref, x_ref.at[pl.ds(0, rows), target], sem.at[d, 3]))
        for copy in found:
            copy.start()
        waiting.append(found)
    columns = pl.ds(pl.multiple_of(core * rows, B), rows)
    trailing = pltpu.make_async_copy(upd_ref.at[:, columns], t_ref, sems.at[0])
    trailing.start()

    def ready(k):
        for copy in waiting[k]:
            copy.wait()

    def done(k, f):
        @pl.when(col == k)
        def _():
            fb_ref[...] = f[0:rows]

    solve_rows(x_ref, fh_ref, fl_ref, u0_ref, u1_ref, v_ref, ready, done)
    out = [
        pltpu.make_async_copy(fh_ref.at[pl.ds(0, rows)], oh_ref, sems.at[1]),
        pltpu.make_async_copy(fl_ref.at[pl.ds(0, rows)], ol_ref, sems.at[2]),
    ]
    for copy in out:
        copy.start()
    trailing.wait()
    t_ref[...] = t_ref[...] - dot3(
        dot_nt, (fh_ref[0:rows, :], fl_ref[0:rows, :]), (fh_ref[rows:, :], fl_ref[rows:, :])
    )
    out.append(pltpu.make_async_copy(t_ref, part_ref, sems.at[3]))
    out[-1].start()
    for copy in out:
        copy.wait()


def solve_last(
    idx_ref, other_ref, oh_ref, ol_ref, part_ref, top0_ref, top1_ref, w0_ref, w1_ref, upd_ref, map_ref,
    schur_ref, send_ref,
    x_ref, u0_ref, u1_ref, v_ref, fh_ref, fl_ref, rh_ref, rl_ref, t_ref, o_ref, sem, sems,
):
    row, core, side, leaf = idx_ref[0], idx_ref[2], idx_ref[3], idx_ref[5]
    ncol, rows, width = other_ref.shape
    waiting = []
    for y in range(ncol):
        found = load_factor(y, top0_ref, top1_ref, w0_ref, w1_ref, u0_ref, u1_ref, v_ref, sem)
        found.append(pltpu.make_async_copy(other_ref.at[y], x_ref.at[:, pl.ds(y * width, width)], sem.at[y, 2]))
        for copy in found:
            copy.start()
        waiting.append(found)
    mine = pl.ds(pl.multiple_of(core * rows, B), rows)
    rest = pl.ds(pl.multiple_of((1 - core) * rows, B), rows)
    later = [
        pltpu.make_async_copy(oh_ref, rh_ref, sems.at[0]),
        pltpu.make_async_copy(ol_ref, rl_ref, sems.at[1]),
        pltpu.make_async_copy(part_ref, t_ref.at[:, mine], sems.at[2]),
        pltpu.make_async_copy(upd_ref.at[:, rest], t_ref.at[:, rest], sems.at[3]),
    ]
    for copy in later:
        copy.start()

    def ready(k):
        for copy in waiting[k]:
            copy.wait()

    solve_rows(x_ref, fh_ref, fl_ref, u0_ref, u1_ref, v_ref, ready, lambda k, f: None)
    for copy in later:
        copy.wait()
    product = dot3(dot_nt, (rh_ref[...], rl_ref[...]), (fh_ref[...], fl_ref[...]))
    t_ref[:, rest] = t_ref[:, rest] - product
    out = pltpu.make_async_copy(t_ref, schur_ref, sems.at[4])
    out.start()
    half = o_ref.shape[0]
    place = lax.broadcasted_iota(jnp.int32, (half, rows), 0) + (row * 2 + 1 - side) * half
    row_map = map_ref[pl.ds(leaf, 1), pl.ds(pl.multiple_of(row * rows, B), rows)]
    onehot = (place == row_map).astype(F32).astype(BF16)
    o_ref[...] = pick_rows(onehot, split3(t_ref[...]))
    sent = pltpu.make_async_copy(o_ref, send_ref, sems.at[5])
    sent.start()
    out.wait()
    sent.wait()


def widen(value, maps, first, base, split):
    blocks = len(maps)
    width = value.shape[1] // blocks
    total = first.shape[1]
    step = total // blocks
    for b in range(blocks):
        lo = b * step // B * B
        hi = -((-(b + 1) * step) // B) * B
        place = lax.broadcasted_iota(jnp.int32, (hi - lo, width), 0) + (lo + base)
        onehot = (place == maps[b]).astype(F32).astype(BF16)
        first[:, lo:hi] = first[:, lo:hi] + pick_cols(split(value[:, b * width : (b + 1) * width]), onehot)


def col_maps(map_ref, leaf, col, rows, cols):
    return [
        map_ref[pl.ds(leaf, 1), pl.ds(pl.multiple_of(col * cols + b * rows, B), rows)] for b in range(cols // rows)
    ]


def own_kernel(idx_ref, schur_ref, map_ref, diag_ref, o_ref):
    row, col, side, leaf = idx_ref[0], idx_ref[1], idx_ref[3], idx_ref[5]
    half, total = o_ref.shape
    rows, cols = schur_ref.shape
    rid = lax.broadcasted_iota(jnp.int32, (half, total), 0) + (row * 2 + side) * half
    cid = lax.broadcasted_iota(jnp.int32, (half, total), 1) + col * total
    o_ref[...] = jnp.where(rid == cid, diag_ref[...], 0.0)
    place = lax.broadcasted_iota(jnp.int32, (half, rows), 0) + (row * 2 + side) * half
    row_map = map_ref[pl.ds(leaf, 1), pl.ds(pl.multiple_of(row * rows, B), rows)]
    onehot = (place == row_map).astype(F32).astype(BF16)
    maps = col_maps(map_ref, leaf, col, rows, cols)
    widen(pick_rows(onehot, split3(schur_ref[...])), maps, o_ref, col * total, split3)


def add_kernel(rows, idx_ref, got_ref, map_ref, base_ref, o_ref):
    side, leaf, col = idx_ref[3], idx_ref[5], idx_ref[1]
    o_ref[...] = base_ref[...]
    maps = col_maps(map_ref, leaf + 1 - 2 * side, col, rows, got_ref.shape[1])
    widen(got_ref[...], maps, o_ref, col * o_ref.shape[1], split2)


def on_device(pivot, border, update, child_map, parent_diag):
    nrow, ncol = lax.axis_size("row"), lax.axis_size("col")
    row, col, leaf = lax.axis_index("row"), lax.axis_index("col"), lax.axis_index("leaf")
    nx = nrow // 2
    core, side = row % 2, leaf % 2
    idx = jnp.stack([row, col, core, side, jnp.int32(ncol), leaf]).astype(jnp.int32)
    piece_rows, piece_cols = pivot.shape[1:]
    n = piece_rows * nrow
    rows, width = border.shape[1:]
    half = parent_diag.shape[1]
    total = 2 * half * nrow // ncol
    upd_cols = update.shape[2]

    chips = nx * ncol
    packed = pl.pallas_call(
        pack_kernel,
        out_shape=jax.ShapeDtypeStruct((chips, PAYLOAD, B), F32),
        in_specs=[SMEM, VMEM],
        out_specs=VMEM,
        **params(10**6),
    )(idx, pivot[0])
    groups = [[(2 * x + c) * ncol + y for x in range(nx) for y in range(ncol)] for c in range(2)]
    mine = lax.all_to_all(packed, ("row", "col"), 0, 0, axis_index_groups=groups, tiled=True)
    swap = [(r, r ^ 1) for r in range(nrow)]

    turn = [((2 * x + c) * ncol + y, (2 * y + c) * ncol + x) for x in range(nx) for c in range(2) for y in range(ncol)]
    bord, mine = lax.optimization_barrier((border[0], mine))
    turned = lax.ppermute(bord, ("row", "col"), turn)
    other = lax.ppermute(mine, "row", swap)
    own = [lax.ppermute(bord, "col", [(y, (y + d) % ncol) for y in range(ncol)]) for d in range(1, ncol)]

    def factor(kernel, order, count, operands, specs, work):
        left = order - 2 * B * count
        shapes = [jax.ShapeDtypeStruct((2 * B * count, order), F32)]
        if left:
            shapes.append(jax.ShapeDtypeStruct((left, left), F32))
        shapes += [
            jax.ShapeDtypeStruct((count, 2 * B, 2 * B), F32),
            jax.ShapeDtypeStruct((piece_rows, piece_cols), F32),
        ]
        return pl.pallas_call(
            kernel,
            out_shape=tuple(shapes),
            in_specs=[SMEM] + specs,
            out_specs=tuple([HBM] * (len(shapes) - 1) + [VMEM]),
            scratch_shapes=[
                pltpu.VMEM((order, order), F32),
                pltpu.VMEM((count, 2 * B, 2 * B), F32),
                pltpu.VMEM((B, 2 * B), F32),
                pltpu.SemaphoreType.DMA((3,)),
            ],
            **params(work, 58),
        )(idx, *operands)

    early = n // (4 * B)
    late = n // (2 * B) - early
    top0, rest, inv0, block = factor(chol_first, n, early, (mine, other), [VMEM, VMEM], 2 * 10**10)

    turned, rest, *own = lax.optimization_barrier((turned, rest, *own))
    same = [[2 * x + c for x in range(nx)] for c in range(2)]
    col_mine = lax.all_to_all(
        jnp.broadcast_to(turned, (nx, rows, width)), "row", 0, 0, axis_index_groups=same, tiled=True
    )
    top1, inv1, pivot_out = factor(
        functools.partial(chol_next, early), 2 * B * late, late, (rest, block), [HBM, VMEM], 2 * 10**10
    )

    col_mine, inv1 = lax.optimization_barrier((col_mine, inv1))
    col_other = lax.ppermute(col_mine, "row", swap)
    half_f = jax.ShapeDtypeStruct((rows, n), BF16)
    factor_refs = [pltpu.VMEM(top0.shape, F32), pltpu.VMEM(top1.shape, F32), pltpu.VMEM((ncol, 2 * B, 2 * B), F32)]
    border_out, own_high, own_low, part = pl.pallas_call(
        solve_first,
        out_shape=(
            jax.ShapeDtypeStruct((rows, width), F32),
            half_f,
            half_f,
            jax.ShapeDtypeStruct((rows, rows), F32),
        ),
        in_specs=[SMEM] + [HBM] * 10,
        out_specs=(VMEM, HBM, HBM, HBM),
        scratch_shapes=[pltpu.VMEM((2 * rows, n), F32)]
        + factor_refs
        + [
            pltpu.VMEM((2 * rows, n), BF16),
            pltpu.VMEM((2 * rows, n), BF16),
            pltpu.VMEM((rows, rows), F32),
            pltpu.SemaphoreType.DMA((ncol, 4)),
            pltpu.SemaphoreType.DMA((4,)),
        ],
        **params(10**10),
    )(idx, bord, *own, col_mine, top0, top1, inv0, inv1, update[0])
    schur, send = pl.pallas_call(
        solve_last,
        out_shape=(
            jax.ShapeDtypeStruct((rows, upd_cols), F32),
            jax.ShapeDtypeStruct((half, upd_cols), F32),
        ),
        in_specs=[SMEM] + [HBM] * 9 + [VMEM],
        out_specs=(HBM, HBM),
        scratch_shapes=[pltpu.VMEM((rows, n), F32)]
        + factor_refs
        + [pltpu.VMEM((rows, n), BF16)] * 4
        + [
            pltpu.VMEM((rows, upd_cols), F32),
            pltpu.VMEM((half, upd_cols), F32),
            pltpu.SemaphoreType.DMA((ncol, 3)),
            pltpu.SemaphoreType.DMA((6,)),
        ],
        **params(10**10),
    )(idx, col_other, own_high, own_low, part, top0, top1, inv0, inv1, update[0], child_map)

    got = lax.ppermute(send, "leaf", [(s, s ^ 1) for s in range(lax.axis_size("leaf"))])
    base = pl.pallas_call(
        own_kernel,
        out_shape=jax.ShapeDtypeStruct((half, total), F32),
        in_specs=[SMEM] + [VMEM] * 3,
        out_specs=VMEM,
        **params(2 * 10**9, 16),
    )(idx, schur, child_map, parent_diag.reshape(half, 1))
    parent_out = pl.pallas_call(
        functools.partial(add_kernel, rows),
        out_shape=jax.ShapeDtypeStruct((half, total), F32),
        in_specs=[SMEM] + [VMEM] * 3,
        out_specs=VMEM,
        **params(2 * 10**9, 16),
    )(idx, got, child_map, base)
    return pivot_out[None], border_out[None], parent_out[None]


def solution(mesh):
    placed = (
        P("leaf", "row", "col"),
        P("leaf", "row", "col"),
        P("leaf", "row", "col"),
        P(),
        P("leaf", "row"),
    )
    return jax.shard_map(
        on_device,
        mesh=mesh,
        in_specs=placed,
        out_specs=(P("leaf", "row", "col"), P("leaf", "row", "col"), P("leaf", "row", "col")),
        check_vma=False,
    )
```

```python
import functools

import jax
import jax.numpy as jnp
from jax import lax
from jax.experimental import pallas as pl
from jax.experimental.pallas import tpu as pltpu
from jax.sharding import PartitionSpec as P

HI = lax.Precision.HIGHEST
F32 = jnp.float32
BF16 = jnp.bfloat16
B = 128
SB = 32
H = 64
PAYLOAD = 144
VMEM = pl.BlockSpec(memory_space=pltpu.VMEM)
HBM = pl.BlockSpec(memory_space=pltpu.HBM)
SMEM = pl.BlockSpec(memory_space=pltpu.SMEM)


def dot_tn(a, b, precision=HI):
    return lax.dot_general(a, b, (((0,), (0,)), ((), ())), precision=precision, preferred_element_type=F32)


def dot_nn(a, b, precision=HI):
    return lax.dot_general(a, b, (((1,), (0,)), ((), ())), precision=precision, preferred_element_type=F32)


def dot_nt(a, b, precision=HI):
    return lax.dot_general(a, b, (((1,), (1,)), ((), ())), precision=precision, preferred_element_type=F32)


def params(flops, mib=60):
    return dict(
        compiler_params=pltpu.CompilerParams(vmem_limit_bytes=mib * 2**20),
        cost_estimate=pl.CostEstimate(flops=flops, bytes_accessed=2**23, transcendentals=0),
    )


def pack_kernel(idx_ref, p_ref, o_ref):
    row, col = idx_ref[0], idx_ref[1]
    copies = o_ref.shape[0]

    def put(lo, value):
        for q in range(copies):
            o_ref[q, lo : lo + value.shape[0], :] = value

    for half in range(2):
        block = p_ref[:, half * B : half * B + B]
        other = 2 * col + half

        @pl.when(row < other)
        def _():
            put(half * H, block[0:H, :])

        @pl.when(row > other)
        def _():
            put(half * H, block[:, H:B].T)

        @pl.when(row == other)
        def _():
            q = H // 2
            put(half * H, block[0:q, :])
            put(half * H + q, jnp.concatenate([block[H : H + q, H : H + q], block[q:H, q:B]], axis=1))
            side = jnp.concatenate([block[H : H + q, H + q : B], block[H + q : B, H + q : B]], axis=1)
            put(2 * H, jnp.concatenate([side[0 : q // 2], side[q // 2 : q]], axis=1))


def unpack(src, parity, u_ref, nrow, ncol):
    for x in range(nrow // 2):
        i = 2 * x + parity
        for y in range(ncol):
            c = x * ncol + y
            for half in range(2):
                o = 2 * y + half
                piece = src[c, half * H : half * H + H, :]
                if i < o:
                    u_ref[i * B : i * B + H, o * B : o * B + B] = piece
                elif i > o:
                    u_ref[o * B + H : o * B + B, i * B : i * B + B] = piece
                else:
                    q = H // 2
                    u_ref[i * B : i * B + q, i * B : i * B + B] = piece[0:q]
                    u_ref[i * B + q : i * B + H, i * B : i * B + B] = jnp.concatenate(
                        [piece[0:q, q:H].T, piece[q:H, q:B]], axis=1
                    )
                    side = src[c, 2 * H : 2 * H + q // 2, :]
                    side = jnp.concatenate([side[:, 0:H], side[:, H:B]], axis=0)
                    right = jnp.concatenate(
                        [
                            jnp.concatenate([piece[q:H, 0:q], side[:, 0:q]], axis=1),
                            jnp.concatenate([side[:, 0:q].T, side[:, q:H]], axis=1),
                        ],
                        axis=0,
                    )
                    cross = jnp.concatenate([piece[0:q, H:B], piece[q:H, H:B]], axis=0).T
                    u_ref[i * B + H : i * B + B, i * B : i * B + B] = jnp.concatenate([cross, right], axis=1)


def spread_row(value, r):
    return jnp.broadcast_to(value[r : r + 1, :], (8, B))


def chain(s_ref, s):
    nb, r0 = SB // 8, s * SB
    rowid = lax.broadcasted_iota(jnp.int32, (8, B), 0)
    blk = [s_ref[r0 + 8 * b : r0 + 8 * b + 8, 0:B] for b in range(nb)]
    c = [
        [
            jnp.broadcast_to(blk[b][:, r0 + i : r0 + i + 1], (8, B)) if b >= i // 8 else None
            for b in range(nb)
        ]
        for i in range(SB)
    ]
    x = [[s_ref[r0 + 8 * b : r0 + 8 * b + 8, B * h : B * h + B] for h in range(2)] for b in range(nb)]
    pivots = [None] * nb
    for j in range(SB):
        bj, rj = j // 8, j % 8
        p = spread_row(c[j][bj], rj)
        inv = 1.0 / p
        pivots[bj] = p if pivots[bj] is None else jnp.where(rowid == rj, p, pivots[bj])
        for i in range(j + 1, SB):
            m = spread_row(c[j][i // 8], i % 8) * inv
            for b in range(i // 8, nb):
                c[i][b] = c[i][b] - c[j][b] * m
        for h in range(2):
            xr = spread_row(x[bj][h], rj) * inv
            for b in range(bj, nb):
                cm = c[j][b] if b > bj else jnp.where(rowid > rj, c[j][b], 0.0)
                x[b][h] = x[b][h] - cm * xr
    out = []
    for b in range(nb):
        q = lax.rsqrt(pivots[b])
        out.append(jnp.concatenate([x[b][0] * q, x[b][1] * q], axis=1))
    return jnp.concatenate(out, axis=0)


def factor_block(s_ref):
    for q in range(B // SB):
        p = chain(s_ref, q)
        s_ref[SB * q : SB * q + SB, :] = p
        below = SB * (q + 1)
        if below < B:
            s_ref[below:, :] = s_ref[below:, :] - dot_tn(p[:, below:B], p)


def chol_steps(u_ref, w_ref, s_ref, steps):
    n = u_ref.shape[0]
    ri = lax.broadcasted_iota(jnp.int32, (B, B), 0)
    ci = lax.broadcasted_iota(jnp.int32, (B, B), 1)
    eye = (ri == ci).astype(F32)

    def body(k, _):
        r0 = pl.multiple_of(k * B, B)
        s_ref[:, 0:B] = u_ref[pl.ds(r0, B), pl.ds(r0, B)]
        s_ref[:, B : 2 * B] = eye
        factor_block(s_ref)
        w = s_ref[:, B : 2 * B]
        for kk in range(steps):

            @pl.when(k == kk)
            def _():
                lo = (kk + 1) * B
                u_ref[kk * B : lo, kk * B : lo] = jnp.where(ri <= ci, s_ref[:, 0:B], 0.0)
                place = slice(kk % 2 * B, kk % 2 * B + B)
                w_ref[kk // 2, place, place] = w
                if lo < n:
                    panel = dot_nn(w, u_ref[kk * B : lo, lo:])
                    u_ref[kk * B : lo, lo:] = panel
                    for t in range(lo, n, 2 * B):
                        m = min(2 * B, n - t)
                        u_ref[t : t + m, t:] = u_ref[t : t + m, t:] - dot_tn(
                            panel[:, t - lo : t - lo + m], panel[:, t - lo :]
                        )

        return 0

    lax.fori_loop(0, steps, body, 0)
    for pair in range(steps // 2):
        lo = 2 * pair * B
        cross = dot_tn(u_ref[lo : lo + B, lo + B : lo + 2 * B], w_ref[pair, 0:B, 0:B])
        w_ref[pair, B : 2 * B, 0:B] = -dot_nn(w_ref[pair, B : 2 * B, B : 2 * B], cross)
        w_ref[pair, 0:B, B : 2 * B] = jnp.zeros((B, B), F32)


def lower_block(u_ref, l_ref, row, first_col, col):
    rows, cols = l_ref.shape
    start = pl.multiple_of((col - first_col) * cols, B)
    part = u_ref[pl.ds(start, cols), pl.ds(pl.multiple_of(row * rows - first_col * cols, B), rows)].T
    rl = lax.broadcasted_iota(jnp.int32, (rows, cols), 0) + row * rows
    cl = lax.broadcasted_iota(jnp.int32, (rows, cols), 1) + col * cols
    l_ref[...] = jnp.where(rl >= cl, part, 0.0)


def copy_all(sources, targets, sems):
    copies = [pltpu.make_async_copy(s, t, sems.at[i]) for i, (s, t) in enumerate(zip(sources, targets))]
    for copy in copies:
        copy.start()
    return copies


def chol_first(idx_ref, mine_ref, other_ref, top_ref, rest_ref, w_ref, l_ref, u_ref, v_ref, s_ref, sems):
    row, col, core = idx_ref[0], idx_ref[1], idx_ref[2]
    nblk = u_ref.shape[0] // B
    ncol = mine_ref.shape[0] // (nblk // 2)
    for parity in range(2):

        @pl.when(core == parity)
        def _():
            unpack(mine_ref, parity, u_ref, nblk, ncol)
            unpack(other_ref, 1 - parity, u_ref, nblk, ncol)

    chol_end(u_ref, v_ref, s_ref, sems, top_ref, rest_ref, w_ref, l_ref, row, col, 0)


def chol_next(first_col, idx_ref, from_ref, before_ref, *refs):
    top_ref, w_ref, l_ref, u_ref, v_ref, s_ref, sems = refs
    copy_all((from_ref,), (u_ref,), sems)[0].wait()
    l_ref[...] = before_ref[...]
    chol_end(u_ref, v_ref, s_ref, sems, top_ref, None, w_ref, l_ref, idx_ref[0], idx_ref[1], first_col)


def chol_end(u_ref, v_ref, s_ref, sems, top_ref, rest_ref, w_ref, l_ref, row, col, first_col):
    count = w_ref.shape[0]
    done = count * 2 * B
    left = u_ref.shape[0] - done
    chol_steps(u_ref, v_ref, s_ref, count * 2)
    sources, targets = (v_ref, u_ref.at[pl.ds(0, done)]), (w_ref, top_ref)
    if left > 0:
        sources += (u_ref.at[pl.ds(done, left), pl.ds(done, left)],)
        targets += (rest_ref,)
    copies = copy_all(sources, targets, sems)
    rows, cols = l_ref.shape
    if first_col == 0:
        l_ref[...] = jnp.zeros_like(l_ref)

    @pl.when((col >= first_col) & (col < first_col + count) & (row * rows >= first_col * cols))
    def _():
        lower_block(u_ref, l_ref, row, first_col, col)

    for copy in copies:
        copy.wait()


def split3(value):
    first = value.astype(BF16)
    rest = value - first.astype(F32)
    second = rest.astype(BF16)
    third = (rest - second.astype(F32)).astype(BF16)
    return first, second, third


def pick_rows(onehot, parts):
    return sum(dot_nn(onehot, part, None) for part in reversed(parts))


def pick_cols(parts, onehot):
    return sum(dot_nt(part, onehot, None) for part in reversed(parts))


def split2(value):
    first = value.astype(BF16)
    return first, (value - first.astype(F32)).astype(BF16)


def dot3(dot, a, b):
    return dot(a[0], b[1], None) + dot(a[1], b[0], None) + dot(a[0], b[0], None)


def solve_kernel(
    idx_ref, own0_ref, own1_ref, own2_ref, own3_ref, mine_ref, other_ref, top0_ref, top1_ref,
    w0_ref, w1_ref, upd_ref, map_ref,
    fb_ref, schur_ref, send_ref,
    x_ref, u0_ref, u1_ref, v_ref, fh_ref, fl_ref, t_ref, o_ref, sem, sems,
):
    row, col, core, side, leaf = idx_ref[0], idx_ref[1], idx_ref[2], idx_ref[3], idx_ref[5]
    ncol, rows, width = mine_ref.shape

    def load(y):
        cols = pl.ds(y * width, width)
        found = []
        if y == 0:
            for d, ref in enumerate((own0_ref, own1_ref, own2_ref, own3_ref)):
                whose = lax.rem(col + ncol - d, ncol)
                target = pl.ds(pl.multiple_of(whose * width, B), width)
                found.append(pltpu.make_async_copy(ref, x_ref.at[pl.ds(0, rows), target], sem.at[d, 0]))
        for c, ref in ((core, mine_ref), (1 - core, other_ref)):
            target = pl.ds(pl.multiple_of((1 + c) * rows, B), rows)
            which = 1 if ref is mine_ref else 2
            found.append(pltpu.make_async_copy(ref.at[y], x_ref.at[target, cols], sem.at[y, which]))
        early = w0_ref.shape[0]
        inverse = w0_ref.at[y] if y < early else w1_ref.at[y - early]
        found.append(pltpu.make_async_copy(inverse, v_ref.at[y], sem.at[y, 3]))
        if y == 0:
            found.append(pltpu.make_async_copy(top0_ref, u0_ref, sem.at[y, 4]))
        if y == 1:
            found.append(pltpu.make_async_copy(top1_ref, u1_ref, sem.at[y, 4]))
        for copy in found:
            copy.start()
        return found

    waiting = [load(y) for y in range(ncol)]
    trailing = pltpu.make_async_copy(upd_ref, t_ref, sems.at[0])
    trailing.start()
    cut = u0_ref.shape[0]
    for k in range(ncol):
        for copy in waiting[k]:
            copy.wait()
        lo, hi = k * width, (k + 1) * width
        x = x_ref[:, lo:hi]
        if k > 0:
            top = min(lo, cut)
            x = x - dot3(dot_nn, (fh_ref[:, 0:top], fl_ref[:, 0:top]), split2(u0_ref[0:top, lo:hi]))
            if lo > cut:
                above = split2(u1_ref[0 : lo - cut, lo - cut : hi - cut])
                x = x - dot3(dot_nn, (fh_ref[:, cut:lo], fl_ref[:, cut:lo]), above)
        f = dot3(dot_nt, split2(x), split2(v_ref[k]))
        fh_ref[:, lo:hi], fl_ref[:, lo:hi] = split2(f)

        @pl.when(col == k)
        def _():
            fb_ref[...] = f[0:rows]

    trailing.wait()
    schur = t_ref[...] - dot3(
        dot_nt, (fh_ref[0:rows, :], fl_ref[0:rows, :]), (fh_ref[rows:, :], fl_ref[rows:, :])
    )
    t_ref[...] = schur
    out = pltpu.make_async_copy(t_ref, schur_ref, sems.at[1])
    out.start()
    half = o_ref.shape[0]
    place = lax.broadcasted_iota(jnp.int32, (half, rows), 0) + (row * 2 + 1 - side) * half
    row_map = map_ref[pl.ds(leaf, 1), pl.ds(pl.multiple_of(row * rows, B), rows)]
    onehot = (place == row_map).astype(F32).astype(BF16)
    o_ref[...] = pick_rows(onehot, split2(schur))
    sent = pltpu.make_async_copy(o_ref, send_ref, sems.at[2])
    sent.start()
    out.wait()
    sent.wait()


def widen(value, maps, first, base, split):
    blocks = len(maps)
    width = value.shape[1] // blocks
    total = first.shape[1]
    step = total // blocks
    for b in range(blocks):
        lo = b * step // B * B
        hi = -((-(b + 1) * step) // B) * B
        place = lax.broadcasted_iota(jnp.int32, (hi - lo, width), 0) + (lo + base)
        onehot = (place == maps[b]).astype(F32).astype(BF16)
        first[:, lo:hi] = first[:, lo:hi] + pick_cols(split(value[:, b * width : (b + 1) * width]), onehot)


def col_maps(map_ref, leaf, col, rows, cols):
    return [
        map_ref[pl.ds(leaf, 1), pl.ds(pl.multiple_of(col * cols + b * rows, B), rows)] for b in range(cols // rows)
    ]


def own_kernel(idx_ref, schur_ref, map_ref, diag_ref, o_ref):
    row, col, side, leaf = idx_ref[0], idx_ref[1], idx_ref[3], idx_ref[5]
    half, total = o_ref.shape
    rows, cols = schur_ref.shape
    rid = lax.broadcasted_iota(jnp.int32, (half, total), 0) + (row * 2 + side) * half
    cid = lax.broadcasted_iota(jnp.int32, (half, total), 1) + col * total
    o_ref[...] = jnp.where(rid == cid, diag_ref[...], 0.0)
    place = lax.broadcasted_iota(jnp.int32, (half, rows), 0) + (row * 2 + side) * half
    row_map = map_ref[pl.ds(leaf, 1), pl.ds(pl.multiple_of(row * rows, B), rows)]
    onehot = (place == row_map).astype(F32).astype(BF16)
    maps = col_maps(map_ref, leaf, col, rows, cols)
    widen(pick_rows(onehot, split3(schur_ref[...])), maps, o_ref, col * total, split3)


def add_kernel(rows, idx_ref, got_ref, map_ref, base_ref, o_ref):
    side, leaf, col = idx_ref[3], idx_ref[5], idx_ref[1]
    o_ref[...] = base_ref[...]
    maps = col_maps(map_ref, leaf + 1 - 2 * side, col, rows, got_ref.shape[1])
    widen(got_ref[...], maps, o_ref, col * o_ref.shape[1], split2)


def on_device(pivot, border, update, child_map, parent_diag):
    nrow, ncol = lax.axis_size("row"), lax.axis_size("col")
    row, col, leaf = lax.axis_index("row"), lax.axis_index("col"), lax.axis_index("leaf")
    nx = nrow // 2
    core, side = row % 2, leaf % 2
    idx = jnp.stack([row, col, core, side, jnp.int32(ncol), leaf]).astype(jnp.int32)
    piece_rows, piece_cols = pivot.shape[1:]
    n = piece_rows * nrow
    rows, width = border.shape[1:]
    half = parent_diag.shape[1]
    total = 2 * half * nrow // ncol
    upd_cols = update.shape[2]

    chips = nx * ncol
    packed = pl.pallas_call(
        pack_kernel,
        out_shape=jax.ShapeDtypeStruct((chips, PAYLOAD, B), F32),
        in_specs=[SMEM, VMEM],
        out_specs=VMEM,
        **params(10**6),
    )(idx, pivot[0])
    groups = [[(2 * x + c) * ncol + y for x in range(nx) for y in range(ncol)] for c in range(2)]
    mine = lax.all_to_all(packed, ("row", "col"), 0, 0, axis_index_groups=groups, tiled=True)
    swap = [(r, r ^ 1) for r in range(nrow)]

    turn = [((2 * x + c) * ncol + y, (2 * y + c) * ncol + x) for x in range(nx) for c in range(2) for y in range(ncol)]
    bord, mine = lax.optimization_barrier((border[0], mine))
    turned = lax.ppermute(bord, ("row", "col"), turn)
    other = lax.ppermute(mine, "row", swap)
    own = [lax.ppermute(bord, "col", [(y, (y + d) % ncol) for y in range(ncol)]) for d in range(1, ncol)]

    def factor(kernel, order, count, operands, specs, work):
        left = order - 2 * B * count
        shapes = [jax.ShapeDtypeStruct((2 * B * count, order), F32)]
        if left:
            shapes.append(jax.ShapeDtypeStruct((left, left), F32))
        shapes += [
            jax.ShapeDtypeStruct((count, 2 * B, 2 * B), F32),
            jax.ShapeDtypeStruct((piece_rows, piece_cols), F32),
        ]
        return pl.pallas_call(
            kernel,
            out_shape=tuple(shapes),
            in_specs=[SMEM] + specs,
            out_specs=tuple([HBM] * (len(shapes) - 1) + [VMEM]),
            scratch_shapes=[
                pltpu.VMEM((order, order), F32),
                pltpu.VMEM((count, 2 * B, 2 * B), F32),
                pltpu.VMEM((B, 2 * B), F32),
                pltpu.SemaphoreType.DMA((3,)),
            ],
            **params(work, 58),
        )(idx, *operands)

    early = n // (4 * B)
    late = n // (2 * B) - early
    top0, rest, inv0, block = factor(chol_first, n, early, (mine, other), [VMEM, VMEM], 2 * 10**10)

    turned, rest, *own = lax.optimization_barrier((turned, rest, *own))
    same = [[2 * x + c for x in range(nx)] for c in range(2)]
    col_mine = lax.all_to_all(
        jnp.broadcast_to(turned, (nx, rows, width)), "row", 0, 0, axis_index_groups=same, tiled=True
    )
    top1, inv1, pivot_out = factor(
        functools.partial(chol_next, early), 2 * B * late, late, (rest, block), [HBM, VMEM], 2 * 10**10
    )

    col_mine, inv1 = lax.optimization_barrier((col_mine, inv1))
    col_other = lax.ppermute(col_mine, "row", swap)
    border_out, schur, send = pl.pallas_call(
        solve_kernel,
        out_shape=(
            jax.ShapeDtypeStruct((rows, width), F32),
            jax.ShapeDtypeStruct((rows, upd_cols), F32),
            jax.ShapeDtypeStruct((half, upd_cols), F32),
        ),
        in_specs=[SMEM] + [HBM] * 11 + [VMEM],
        out_specs=(VMEM, HBM, HBM),
        scratch_shapes=[
            pltpu.VMEM((3 * rows, n), F32),
            pltpu.VMEM(top0.shape, F32),
            pltpu.VMEM(top1.shape, F32),
            pltpu.VMEM((ncol, 2 * B, 2 * B), F32),
            pltpu.VMEM((3 * rows, n), BF16),
            pltpu.VMEM((3 * rows, n), BF16),
            pltpu.VMEM((rows, upd_cols), F32),
            pltpu.VMEM((half, upd_cols), F32),
            pltpu.SemaphoreType.DMA((ncol, 5)),
            pltpu.SemaphoreType.DMA((3,)),
        ],
        **params(10**10, 60),
    )(idx, bord, *own, col_mine, col_other, top0, top1, inv0, inv1, update[0], child_map)

    got = lax.ppermute(send, "leaf", [(s, s ^ 1) for s in range(lax.axis_size("leaf"))])
    base = pl.pallas_call(
        own_kernel,
        out_shape=jax.ShapeDtypeStruct((half, total), F32),
        in_specs=[SMEM] + [VMEM] * 3,
        out_specs=VMEM,
        **params(2 * 10**9, 16),
    )(idx, schur, child_map, parent_diag.reshape(half, 1))
    parent_out = pl.pallas_call(
        functools.partial(add_kernel, rows),
        out_shape=jax.ShapeDtypeStruct((half, total), F32),
        in_specs=[SMEM] + [VMEM] * 3,
        out_specs=VMEM,
        **params(2 * 10**9, 16),
    )(idx, got, child_map, base)
    return pivot_out[None], border_out[None], parent_out[None]


def solution(mesh):
    placed = (
        P("leaf", "row", "col"),
        P("leaf", "row", "col"),
        P("leaf", "row", "col"),
        P(),
        P("leaf", "row"),
    )
    return jax.shard_map(
        on_device,
        mesh=mesh,
        in_specs=placed,
        out_specs=(P("leaf", "row", "col"), P("leaf", "row", "col"), P("leaf", "row", "col")),
        check_vma=False,
    )
```
